32 devices in a mesh: subj: 8 (over z, x), space: 4 (over y, core).
Axes of the slice: x: 2, y: 2, z: 4, core: 2. Of those that a mesh axis runs over, the one named last changes fastest.
Arguments:
- template_warped: bfloat16 [16, 256, 256, 256], P('subj', 'space'), may hold values from -6 to 6
- subject_images: bfloat16 [16, 256, 256, 256], P('subj', 'space'), may hold values from -5 to 5.5, as said below
- jacobians: bfloat16 [16, 256, 256, 256], P('subj', 'space'), may hold values from 0.29882812 to 3
- velocity: float32 [256, 256, 256], P('space', 'subj'), may hold values from -6 to 6
Outputs:
- velocity_new: float32 [256, 256, 256], P('space', 'subj')
The draws below stay inside these ranges and needn't reach their ends.
Inputs may be any that keep to these rules, and one draw needn't show every extreme that they name: `subject_images`: intensities of the subjects' scans.
All inputs are finite; a program needn't handle non-finite values.
Results may differ from the reference program's by a relative error of at most 0.0003.
Values sent between devices are 32-bit elements; how exact they have to be, the bound alone decides.
No kernel may reach another device: no remote copies, remote signals or barrier semaphores. Data moves between devices by JAX's collectives and lax.ppermute only.
A program may use at most 256 MiB of HBM per device.

```python
import math
import jax
import jax.numpy as jnp
from jax import lax

GRID = 256
SUBJECTS = 16


def draw_subject_images(key, part):
    noise = jax.random.normal(key, (SUBJECTS, GRID, GRID, GRID), jnp.float32)
    noise = jnp.clip(noise, -5.0, 5.0)
    values = noise
    return values.astype(jnp.bfloat16)


def level_of(rng, extent, cuts, least, largest):
    def one(axis_at, blocks):
        draws = jax.random.uniform(jax.random.fold_in(jax.random.fold_in(rng, 6), axis_at), (blocks,), jnp.float32, least / len(cuts), largest / len(cuts))
        return jnp.repeat(jnp.exp(draws), extent[axis_at] // blocks).reshape((-1,) + (1,) * (len(extent) - axis_at - 1))

    loudness = one(*cuts[0])
    for cut in cuts[1:]:
        loudness = loudness * one(*cut)
    return loudness


def bell_draw(key, extent, scale, most, split=(), held_as=jnp.bfloat16):
    loudness = level_of(key, extent, split, -0.22, 0.18) if split else 1.0
    array = jax.random.normal(key, extent, jnp.float32) * scale * loudness
    return jnp.minimum(jnp.maximum(array, -most), most).astype(held_as)


def setup_inputs(seed: int = 0) -> dict:
    splits = jax.random.split(jax.random.key(seed), 5)
    template_warped = bell_draw(splits[0], (SUBJECTS, GRID, GRID, GRID), 1.0, 6.0, ((0, 8), (1, 4)))
    subject_images = draw_subject_images(jax.random.fold_in(splits[4], 71), 0)
    jacobians = jnp.clip(jnp.exp(math.log(3.0) - 2.306499 * jax.random.uniform(splits[2], (SUBJECTS, GRID, GRID, GRID), jnp.float32) ** level_of(splits[2], (SUBJECTS, GRID, GRID, GRID), ((0, 8), (1, 4)), -0.2, 0.2)), 0.29882812, 3.0).astype(jnp.bfloat16)
    velocity = bell_draw(splits[3], (GRID, GRID, GRID), 1.0, 6.0, ((0, 4), (1, 8)), jnp.float32)
    return {"template_warped": template_warped, "subject_images": subject_images, "jacobians": jacobians, "velocity": velocity}


sigma_sq = 0.05
step_size = 0.25
alpha_reach = 16.0


def smoothing_symbol(first, second, third, length):
    def damping(freq):
        turns = (freq % length).astype(jnp.float32)
        return 2.0 - 2.0 * jnp.cos(turns * (2.0 * math.pi / length))
    total = damping(first) + damping(second) + damping(third)
    return 1.0 / (1.0 + alpha_reach * total) ** 2


def reference(template_warped, subject_images, jacobians, velocity):
    length = template_warped.shape[3]

    def add_subject(total, items):
        warped, image, jac = items
        warped32 = warped.astype(jnp.float32)
        slope = (jnp.roll(warped32, -1, axis=2) - jnp.roll(warped32, 1, axis=2)) * 0.5
        term = jac.astype(jnp.float32) * (image.astype(jnp.float32) - warped32) * slope
        return total + term, None

    start = jnp.zeros((length, length, length), jnp.float32)
    total, _ = lax.scan(add_subject, start, (template_warped, subject_images, jacobians))
    force = total * (2.0 / sigma_sq)
    index = jnp.arange(length, dtype=jnp.int32)
    symbol = smoothing_symbol(index[:, None, None], index[None, :, None], index[None, None, :], length)
    spectrum = jnp.fft.fftn(force)
    smoothed = jnp.real(jnp.fft.ifftn(spectrum * symbol))
    return velocity - step_size * (2.0 * velocity - smoothed)
```

```python
import functools
import math

import jax
import jax.numpy as jnp
import ml_dtypes
import numpy as np
from jax import lax
from jax.experimental import pallas as pl
from jax.experimental.pallas import tpu as pltpu
from jax.sharding import PartitionSpec as P

sigma_sq = 0.05
step_size = 0.25
alpha_reach = 16.0
highest = lax.Precision.HIGHEST
vmem_bytes = 30 * 1024 * 1024
lane = 128
chunk_eighths = (4, 3, 1)


def split_bf16(table):
    high = table.astype(ml_dtypes.bfloat16)
    low = (table - high.astype(np.float64)).astype(ml_dtypes.bfloat16)
    return high, low


def packed_np(length):
    half = length // 2
    index = np.arange(length)
    freq = np.where(index <= half, index, index - half)
    angle = (index[:, None] * freq[None, :] % length) * (2.0 * math.pi / length)
    forward = np.where(index[None, :] <= half, np.cos(angle), np.sin(angle))
    weight = np.where((index == 0) | (index == half), 1.0, 2.0) / length
    lam = 2.0 - 2.0 * np.cos(freq * (2.0 * math.pi / length))
    return forward, (forward * weight[None, :]).T, lam


class Plan:
    def __init__(self, length, rows_x, subj, space):
        self.length, self.xl, self.subj, self.space = length, rows_x, subj, space
        self.yl = length // subj
        self.lanes = self.yl * self.xl
        self.half = self.lanes // 2
        self.ty = lane // self.xl if self.xl < lane else 1
        self.tiles = self.lanes // lane
        eighth = length // 8
        self.chunks = [e * eighth for e in chunk_eighths]
        self.offs = np.concatenate([[0], np.cumsum(self.chunks)])[:-1].tolist()
        self.groups = [c // space for c in self.chunks]
        ring = list(range(0, subj, 2)) + list(range(subj - 1, 0, -2))
        self.ring = ring
        self.place = [ring.index(j) for j in range(subj)]
        forward, inverse, lam = packed_np(length)
        order = np.stack(
            [
                np.concatenate(
                    [
                        off + (s ^ d) * g + np.arange(g)
                        for off, g in zip(self.offs, self.groups)
                        for d in range(space)
                    ]
                )
                for s in range(space)
            ]
        )
        high, low = split_bf16(forward.T)
        self.t_table = np.concatenate([high, high, low], axis=1)[order]
        high, low = split_bf16(inverse)
        self.i_table = np.stack([high, low], 0)[:, order].transpose(1, 0, 2, 3)
        eye = np.eye(self.ty)
        blocks = forward.reshape(space, self.xl, length)
        wide = np.einsum("ab,sxw->saxbw", eye, blocks).reshape(space, lane, self.ty * length)
        high, low = split_bf16(wide)
        self.w_table = np.concatenate([high, high, low], axis=1)
        blocks = inverse.reshape(length, space, self.xl)
        wide = np.einsum("ab,wsx->sawbx", eye, blocks).reshape(space, self.ty * length, lane)
        high, low = split_bf16(wide)
        self.v_table = np.concatenate([high, high, low], axis=1)
        index = np.arange(length)
        slope = np.zeros((length, length))
        slope[(index + 1) % length, index] += 0.5
        slope[(index - 1) % length, index] -= 0.5
        self.d_table = slope.astype(ml_dtypes.bfloat16)
        centre = (1.0 + alpha_reach * (lam[:, None] + lam[None, :])) / alpha_reach + 2.0
        r = 2.0 / (centre + np.sqrt(centre * centre - 4.0))
        q = r * r
        scale = (2.0 / sigma_sq) * q / (alpha_reach * alpha_reach)
        self.r_table = np.stack(
            [r, scale * (1 + q) / (1 - q) ** 3, scale / (1 - q) ** 2, np.log(r)]
        ).astype(np.float32)


def split(value):
    high = value.astype(jnp.bfloat16)
    low = (value - high.astype(jnp.float32)).astype(jnp.bfloat16)
    return high, low


def params(**kw):
    return pltpu.CompilerParams(vmem_limit_bytes=vmem_bytes, **kw)


def force_kernel(plan, step_x, place_ref, warped, images, jac, d_ref, t_ref, *rest):
    outs, field = rest[:-1], rest[-1]
    n = len(plan.chunks)
    way, at = pl.program_id(0), pl.program_id(1)
    yh = plan.yl // 2
    count = warped.shape[0]
    length = plan.length
    rows = step_x * yh

    total = None
    for b in range(count):
        w = warped[b].reshape(rows, length)
        slope = jnp.dot(w, d_ref[...], preferred_element_type=jnp.float32)
        diff = images[b].reshape(rows, length).astype(jnp.float32) - w.astype(jnp.float32)
        term = jac[b].reshape(rows, length).astype(jnp.float32) * diff * slope
        total = term if total is None else total + term
    start = pl.multiple_of(at * rows, rows)
    for h in range(length // lane):
        field[h, pl.ds(start, rows), :] = total[:, h * lane : (h + 1) * lane]

    def transform(refs):
        per = max(1, 256 // plan.xl)
        for y0 in range(0, yh, per):
            lines = jnp.concatenate(
                [
                    jnp.concatenate(
                        [
                            field[h, pl.ds(y, plan.xl, stride=yh), :]
                            for h in range(length // lane)
                        ],
                        axis=1,
                    )
                    for y in range(y0, y0 + per)
                ],
                axis=0,
            )
            high, low = split(lines)
            both = jnp.concatenate([high, low, high], axis=1)
            out = lax.dot_general(
                t_ref[0], both, (((1,), (1,)), ((), ())), preferred_element_type=jnp.float32
            )
            for ref, off, size in zip(refs, plan.offs, plan.chunks):
                ref[:, y0 * plan.xl : (y0 + per) * plan.xl] = out[off : off + size]

    last = at == pl.num_programs(1) - 1

    @pl.when(jnp.logical_and(last, way == 0))
    def _():
        transform(outs[:n])

    @pl.when(jnp.logical_and(last, way == 1))
    def _():
        transform(outs[n:])


def force_blocks(plan, place, warped, images, jac):
    count, xl, _, length = warped.shape
    yh = plan.yl // 2
    step_x = min(16, xl)
    source = pl.BlockSpec(
        (count, step_x, yh, length), lambda way, at, place: (0, at, 2 * place[way] + way, 0)
    )
    shapes = [jax.ShapeDtypeStruct((c, plan.half), jnp.float32) for c in plan.chunks] * 2
    outs = pl.pallas_call(
        functools.partial(force_kernel, plan, step_x),
        out_shape=shapes,
        grid_spec=pltpu.PrefetchScalarGridSpec(
            num_scalar_prefetch=1,
            grid=(2, xl // step_x),
            in_specs=[
                source,
                source,
                source,
                pl.BlockSpec((length, length), lambda way, at, place: (0, 0)),
                pl.BlockSpec((1, length, 3 * length), lambda way, at, place: (place[2], 0, 0)),
            ],
            out_specs=[pl.BlockSpec(s.shape, lambda way, at, place: (0, 0)) for s in shapes],
            scratch_shapes=[pltpu.VMEM((length // lane, xl * yh, lane), jnp.float32)],
        ),
        compiler_params=params(),
        cost_estimate=pl.CostEstimate(
            flops=16 * xl * yh * length * length,
            bytes_accessed=12 * count * xl * yh * length + 8 * xl * yh * length,
            transcendentals=0,
        ),
        name="force",
    )(place, warped, images, jac, jnp.asarray(plan.d_table), jnp.asarray(plan.t_table))
    n = len(plan.chunks)
    return outs[:n], outs[n:]


def join_kernel(plan, g, right, right_local, left, left_local, *outs):
    for d, out in enumerate(outs):
        rows = slice(d * g, (d + 1) * g)
        out[:, : plan.half] = right[rows] + right_local[rows]
        out[:, plan.half :] = left[rows] + left_local[rows]


def join(plan, g, right, right_local, left, left_local):
    return pl.pallas_call(
        functools.partial(join_kernel, plan, g),
        out_shape=[jax.ShapeDtypeStruct((g, plan.lanes), jnp.float32)] * plan.space,
        compiler_params=params(),
        name="join",
    )(right, right_local, left, left_local)


def forward_kernel(plan, g, place_ref, w_ref, r_ref, *rest):
    pieces, f_ref, ends_ref = rest[: plan.space], rest[-2], rest[-1]
    me = place_ref[0]
    total = None
    for d, piece in enumerate(pieces):
        lines = jnp.concatenate(
            [piece[:, t * lane : (t + 1) * lane] for t in range(plan.tiles)], axis=0
        )
        high, low = split(lines)
        both = jnp.concatenate([high, low, high], axis=1)
        term = jnp.dot(both, w_ref[me ^ d], preferred_element_type=jnp.float32)
        total = term if total is None else total + term
    f_ref[...] = total
    r = r_ref[0]
    length = plan.length

    def line(y):
        t, a = y // plan.ty, y % plan.ty
        return f_ref[t * g : (t + 1) * g, a * length : (a + 1) * length]

    zero = jnp.zeros_like(r)
    v, w = zero, zero
    for y in range(plan.yl):
        w = r * (w + v)
        v = line(y) + r * v
    ends_ref[0], ends_ref[1] = v, w
    v, w = zero, zero
    for y in range(plan.yl - 1, -1, -1):
        v = v + line(y)
        w = r * (w + v)
        v = r * v
    ends_ref[2], ends_ref[3] = v, w


def forward_lines(plan, g, place, r_tab, pieces):
    rows = plan.tiles * g
    return pl.pallas_call(
        functools.partial(forward_kernel, plan, g),
        out_shape=[
            jax.ShapeDtypeStruct((rows, plan.ty * plan.length), jnp.float32),
            jax.ShapeDtypeStruct((4, g, plan.length), jnp.float32),
        ],
        in_specs=[pl.BlockSpec(memory_space=pltpu.SMEM)]
        + [pl.BlockSpec(memory_space=pltpu.VMEM)] * (2 + plan.space),
        out_specs=[pl.BlockSpec(memory_space=pltpu.VMEM)] * 2,
        compiler_params=params(),
        name="first_forward",
    )(place, jnp.asarray(plan.w_table), r_tab, *pieces)


def combine(ends, other, right, power, span):
    hi = [jnp.where(right, ends[i], other[i]) for i in range(4)]
    lo = [jnp.where(right, other[i], ends[i]) for i in range(4)]
    return (
        hi[0] + power * lo[0],
        hi[1] + power * (lo[1] + span * lo[0]),
        lo[2] + power * hi[2],
        lo[3] + power * (hi[3] + span * hi[2]),
    )


def merge_kernel(plan, stage, place_ref, r_ref, ends_ref, other_ref, out_ref):
    span = float(plan.yl << stage)
    right = (place_ref[0] >> stage) % 2 == 1
    power = jnp.exp(span * r_ref[3])
    ends = [ends_ref[i] for i in range(4)]
    other = [other_ref[i] for i in range(4)]
    for i, value in enumerate(combine(ends, other, right, power, span)):
        out_ref[i] = value


def merge(plan, stage, place, r_tab, ends, other):
    return pl.pallas_call(
        functools.partial(merge_kernel, plan, stage),
        out_shape=jax.ShapeDtypeStruct(ends.shape, jnp.float32),
        in_specs=[pl.BlockSpec(memory_space=pltpu.SMEM)]
        + [pl.BlockSpec(memory_space=pltpu.VMEM)] * 3,
        out_specs=pl.BlockSpec(memory_space=pltpu.VMEM),
        compiler_params=params(),
        name="merge",
    )(place, r_tab, ends, other)


def backward_kernel(plan, g, stages, place_ref, v_ref, r_ref, f_ref, ends_ref, *rest):
    others, outs, u_ref = rest[:stages], rest[stages:-1], rest[-1]
    me, block = place_ref[0], place_ref[1]
    length = plan.length
    r, alpha, beta, log_r = r_ref[0], r_ref[1], r_ref[2], r_ref[3]
    ends = [ends_ref[i] for i in range(4)]
    zero = jnp.zeros_like(r)
    carry = [zero] * 4
    for stage in range(stages):
        other = [others[stage][i] for i in range(4)]
        size = 1 << stage
        right = (block >> stage) % 2 == 1
        inside = block % size
        before = (inside * plan.yl).astype(jnp.float32)
        after = ((size - 1 - inside) * plan.yl).astype(jnp.float32)
        reach = jnp.where(right, before, after)
        power = jnp.exp(reach * log_r)
        for i in (0, 2):
            take = jnp.where(right, 1.0, 0.0) if i == 0 else jnp.where(right, 0.0, 1.0)
            carry[i] = carry[i] + take * (power * other[i])
            carry[i + 1] = carry[i + 1] + take * (power * (other[i + 1] + reach * other[i]))
        if stage == stages - 1:
            span = float(plan.yl << stage)
            ends = combine(ends, other, right, jnp.exp(span * log_r), span)
    full = jnp.exp(float(length) * log_r)
    inverse = 1.0 / (1.0 - full)
    for i in (0, 2):
        v = ends[i] * inverse
        w = (ends[i + 1] + full * (float(length) * v)) * inverse
        reach = (block if i == 0 else plan.subj - 1 - block) * plan.yl
        reach = reach.astype(jnp.float32)
        power = jnp.exp(reach * log_r)
        carry[i] = carry[i] + power * v
        carry[i + 1] = carry[i + 1] + power * (w + reach * v)

    def line(y):
        t, a = y // plan.ty, y % plan.ty
        return (slice(t * g, (t + 1) * g), slice(a * length, (a + 1) * length))

    v, w = carry[0], carry[1]
    for y in range(plan.yl):
        w = r * (w + v)
        v = f_ref[line(y)] + r * v
        u_ref[line(y)] = alpha * v + beta * w
    v, w = carry[2], carry[3]
    for y in range(plan.yl - 1, -1, -1):
        u_ref[line(y)] = u_ref[line(y)] + (alpha * v + beta * w)
        v = v + f_ref[line(y)]
        w = r * (w + v)
        v = r * v
    high, low = split(u_ref[...])
    both = jnp.concatenate([high, low, high], axis=1)
    for d, out in enumerate(outs):
        back = jnp.dot(both, v_ref[me ^ d], preferred_element_type=jnp.float32)
        for t in range(plan.tiles):
            out[:, t * lane : (t + 1) * lane] = back[t * g : (t + 1) * g]


def backward_lines(plan, g, place, r_tab, f, ends, others):
    stages = len(others)
    return pl.pallas_call(
        functools.partial(backward_kernel, plan, g, stages),
        out_shape=[jax.ShapeDtypeStruct((g, plan.lanes), jnp.float32)] * plan.space,
        in_specs=[pl.BlockSpec(memory_space=pltpu.SMEM)]
        + [pl.BlockSpec(memory_space=pltpu.VMEM)] * (4 + stages),
        out_specs=[pl.BlockSpec(memory_space=pltpu.VMEM)] * plan.space,
        scratch_shapes=[pltpu.VMEM(f.shape, jnp.float32)],
        compiler_params=params(),
        name="second_and_back",
    )(place, jnp.asarray(plan.v_table), r_tab, f, ends, *others)


def finish_kernel(plan, y_step, place_ref, i_ref, velocity, *rest):
    pieces, out, field = rest[:-2], rest[-2], rest[-1]
    length, xl = plan.length, plan.xl
    high_table, low_table = i_ref[0, 0], i_ref[0, 1]
    table = jnp.concatenate([high_table, high_table, low_table], axis=0)
    for t in range(y_step // plan.ty):
        columns = jnp.concatenate([p[:, t * lane : (t + 1) * lane] for p in pieces], axis=0)
        high, low = split(columns.T)
        both = jnp.concatenate([high, low, high], axis=1)
        lines = jnp.dot(both, table, preferred_element_type=jnp.float32)
        for a in range(plan.ty):
            y = t * plan.ty + a
            for h in range(length // lane):
                field[h, pl.ds(y, xl, stride=y_step), :] = lines[
                    a * xl : (a + 1) * xl, h * lane : (h + 1) * lane
                ]
    for h in range(length // lane):
        cols = slice(h * lane, (h + 1) * lane)
        vel = velocity[:, :, cols]
        smoothed = field[h].reshape(xl, y_step, lane)
        out[:, :, cols] = vel - step_size * (2.0 * vel - smoothed)


def finish(plan, place, velocity, pieces):
    xl, yl, length = velocity.shape
    y_step = 8
    width = y_step * xl
    return pl.pallas_call(
        functools.partial(finish_kernel, plan, y_step),
        out_shape=jax.ShapeDtypeStruct(velocity.shape, jnp.float32),
        grid_spec=pltpu.PrefetchScalarGridSpec(
            num_scalar_prefetch=1,
            grid=(yl // y_step,),
            in_specs=[
                pl.BlockSpec((1, 2, length, length), lambda at, place: (place[0], 0, 0, 0)),
                pl.BlockSpec((xl, y_step, length), lambda at, place: (0, at, 0)),
            ]
            + [pl.BlockSpec((p.shape[0], width), lambda at, place: (0, at)) for p in pieces],
            out_specs=pl.BlockSpec((xl, y_step, length), lambda at, place: (0, at, 0)),
            scratch_shapes=[pltpu.VMEM((length // lane, xl * y_step, lane), jnp.float32)],
        ),
        compiler_params=params(),
        name="last_back",
    )(place, jnp.asarray(plan.i_table), velocity, *pieces)


def ring_body(plan, template_warped, subject_images, jacobians, velocity):
    subj, space = plan.subj, plan.space
    j, s = lax.axis_index("subj"), lax.axis_index("space")
    ring = jnp.asarray(plan.ring, jnp.int32)
    at = jnp.asarray(plan.place, jnp.int32)[j]
    place = jnp.stack([s, j]).astype(jnp.int32)
    to_right = [(plan.ring[i], plan.ring[(i + 1) % subj]) for i in range(subj)]
    to_left = [(b, a) for a, b in to_right]
    chunks = range(len(plan.chunks))
    r_tabs = [
        lax.dynamic_slice_in_dim(jnp.asarray(plan.r_table), off + s * g, g, axis=1)
        for off, g in zip(plan.offs, plan.groups)
    ]

    local = []
    for k in range(subj):
        blocks = jnp.stack([ring[(at - 1 - k) % subj], ring[(at + 1 + k) % subj], s])
        local.append(
            force_blocks(
                plan, blocks.astype(jnp.int32), template_warped, subject_images, jacobians
            )
        )

    stages = subj.bit_length() - 1
    gate = None
    finished = []
    for c in chunks:
        g = plan.groups[c]
        right, left = local[0][0][c], local[0][1][c]
        if gate is not None:
            right, left, _ = lax.optimization_barrier((right, left, gate))
        for k in range(1, subj):
            right = lax.ppermute(right, "subj", to_right)
            left = lax.ppermute(left, "subj", to_left)
            if k < subj - 1:
                right = right + local[k][0][c]
                left = left + local[k][1][c]
        pieces = join(plan, g, right, local[-1][0][c], left, local[-1][1][c])
        gate = pieces[0]
        pieces = [pieces[0]] + [
            lax.ppermute(pieces[d], "space", [(i, i ^ d) for i in range(space)])
            for d in range(1, space)
        ]
        f, ends = forward_lines(plan, g, place, r_tabs[c], pieces)
        others = []
        for stage in range(stages):
            size = 1 << stage
            other = lax.ppermute(ends, "subj", [(i, i ^ size) for i in range(subj)])
            others.append(other)
            if stage < stages - 1:
                ends = merge(plan, stage, place[1:], r_tabs[c], ends, other)
        pieces = backward_lines(plan, g, place, r_tabs[c], f, ends, others)
        finished += [pieces[0]] + [
            lax.ppermute(pieces[d], "space", [(i, i ^ d) for i in range(space)])
            for d in range(1, space)
        ]
    return finish(plan, place, velocity, finished)


def smoothing_symbol(first, second, third, length):
    def damping(freq):
        turns = (freq % length).astype(jnp.float32)
        return 2.0 - 2.0 * jnp.cos(turns * (2.0 * math.pi / length))

    total = damping(first) + damping(second) + damping(third)
    return 1.0 / (1.0 + alpha_reach * total) ** 2


def transposing_body(template_warped, subject_images, jacobians, velocity):
    length = template_warped.shape[3]
    half = length // 2
    warped = template_warped.astype(jnp.float32)
    slope = (jnp.roll(warped, -1, axis=3) - jnp.roll(warped, 1, axis=3)) * 0.5
    partial_value = jnp.sum(
        jacobians.astype(jnp.float32) * (subject_images.astype(jnp.float32) - warped) * slope,
        axis=0,
    )
    forward, inverse, _ = packed_np(length)
    forward, inverse = forward.astype(np.float32), inverse.astype(np.float32)
    packed = jnp.einsum("xyz,zp->xpy", partial_value, forward, precision=highest)
    packed = lax.psum_scatter(packed, "subj", scatter_dimension=1, tiled=True)
    packed = packed * (2.0 / sigma_sq)
    spectra = jnp.einsum("xpy,yk->kpx", packed, forward, precision=highest)
    lines = lax.all_to_all(spectra, "space", split_axis=0, concat_axis=2, tiled=True)
    freq_lines = jnp.einsum("kpx,xw->kpw", lines, forward, precision=highest)

    def true_freq(index):
        return jnp.where(index <= half, index, index - half)

    def mine(axis, size):
        return true_freq(lax.axis_index(axis) * size + jnp.arange(size, dtype=jnp.int32))

    symbol = smoothing_symbol(
        mine("space", lines.shape[0])[:, None, None],
        mine("subj", lines.shape[1])[None, :, None],
        true_freq(jnp.arange(length, dtype=jnp.int32))[None, None, :],
        length,
    )
    back_lines = jnp.einsum("kpw,wx->xpk", freq_lines * symbol, inverse, precision=highest)
    columns = lax.all_to_all(back_lines, "space", split_axis=0, concat_axis=2, tiled=True)
    real_field = jnp.einsum("xpk,ky->xpy", columns, inverse, precision=highest)
    depth_lines = lax.all_to_all(real_field, "subj", split_axis=2, concat_axis=1, tiled=True)
    smoothed = jnp.einsum("xpy,pz->xyz", depth_lines, inverse, precision=highest)
    return velocity - step_size * (2.0 * velocity - smoothed)


def body(subj, space, template_warped, subject_images, jacobians, velocity):
    _, xl, _, length = template_warped.shape
    yl = velocity.shape[1]
    power_of_two = subj & (subj - 1) == 0 and space & (space - 1) == 0
    fits = (
        subj > 1
        and power_of_two
        and length % lane == 0
        and yl % 32 == 0
        and xl >= 16
        and lane % xl == 0
        and length // 8 // space % 8 == 0
    )
    if not fits:
        return transposing_body(template_warped, subject_images, jacobians, velocity)
    plan = Plan(length, xl, subj, space)
    return ring_body(plan, template_warped, subject_images, jacobians, velocity)


def solution(mesh):
    return jax.shard_map(
        functools.partial(body, mesh.shape["subj"], mesh.shape["space"]),
        mesh=mesh,
        in_specs=(
            P("subj", "space", None, None),
            P("subj", "space", None, None),
            P("subj", "space", None, None),
            P("space", "subj", None),
        ),
        out_specs=P("space", "subj", None),
        check_vma=False,
    )
```

```python
import functools
import math

import jax
import jax.numpy as jnp
import ml_dtypes
import numpy as np
from jax import lax
from jax.experimental import pallas as pl
from jax.experimental.pallas import tpu as pltpu
from jax.sharding import PartitionSpec as P

sigma_sq = 0.05
step_size = 0.25
alpha_reach = 16.0
highest = lax.Precision.HIGHEST
vmem_bytes = 50 * 1024 * 1024
lane = 128
chunk_eighths = (6, 2)
near_step, far_step, ends_step = 3, 4, 5


def split_bf16(table):
    high = table.astype(ml_dtypes.bfloat16)
    low = (table - high.astype(np.float64)).astype(ml_dtypes.bfloat16)
    return high, low


def packed_np(length):
    half = length // 2
    index = np.arange(length)
    freq = np.where(index <= half, index, index - half)
    angle = (index[:, None] * freq[None, :] % length) * (2.0 * math.pi / length)
    forward = np.where(index[None, :] <= half, np.cos(angle), np.sin(angle))
    weight = np.where((index == 0) | (index == half), 1.0, 2.0) / length
    lam = 2.0 - 2.0 * np.cos(freq * (2.0 * math.pi / length))
    return forward, (forward * weight[None, :]).T, lam


class Plan:
    def __init__(self, length, rows_x, subj, space):
        self.length, self.xl, self.subj, self.space = length, rows_x, subj, space
        self.yl = length // subj
        self.lanes = self.yl * self.xl
        self.half = self.lanes // 2
        self.ty = lane // self.xl if self.xl < lane else 1
        self.tiles = self.lanes // lane
        eighth = length // 8
        self.chunks = [e * eighth for e in chunk_eighths]
        self.offs = np.concatenate([[0], np.cumsum(self.chunks)])[:-1].tolist()
        self.groups = [c // space for c in self.chunks]
        ring = list(range(0, subj, 2)) + list(range(subj - 1, 0, -2))
        self.ring = ring
        rows = np.zeros((subj, space, 2 * subj + 2), np.int32)
        for at, j in enumerate(ring):
            for k in range(subj):
                rows[j, :, 2 * k] = ring[(at - 1 - k) % subj]
                rows[j, :, 2 * k + 1] = ring[(at + 1 + k) % subj]
            rows[j, :, 2 * subj] = np.arange(space)
            rows[j, :, 2 * subj + 1] = j
        self.place_table = rows
        self.at_space, self.at_subj = 2 * subj, 2 * subj + 1
        forward, inverse, lam = packed_np(length)
        order = np.stack(
            [
                np.concatenate(
                    [
                        off + (s ^ d) * g + np.arange(g)
                        for off, g in zip(self.offs, self.groups)
                        for d in range(space)
                    ]
                )
                for s in range(space)
            ]
        )
        high, low = split_bf16(forward.T)
        self.t_table = np.concatenate([high, high, low], axis=1)[order]
        high, low = split_bf16(inverse)
        self.i_table = np.stack([high, low], 0)[:, order].transpose(1, 0, 2, 3)
        eye = np.eye(self.ty)
        blocks = forward.reshape(space, self.xl, length)
        wide = np.einsum("ab,sxw->saxbw", eye, blocks).reshape(space, lane, self.ty * length)
        high, low = split_bf16(wide)
        self.w_table = np.concatenate([high, high, low], axis=1)
        blocks = inverse.reshape(length, space, self.xl)
        wide = np.einsum("ab,wsx->sawbx", eye, blocks).reshape(space, self.ty * length, lane)
        high, low = split_bf16(wide)
        self.v_table = np.concatenate([high, high, low], axis=1)
        index = np.arange(length)
        slope = np.zeros((length, length))
        slope[(index + 1) % length, index] += 0.5
        slope[(index - 1) % length, index] -= 0.5
        self.d_table = slope.astype(ml_dtypes.bfloat16)
        centre = (1.0 + alpha_reach * (lam[:, None] + lam[None, :])) / alpha_reach + 2.0
        r = 2.0 / (centre + np.sqrt(centre * centre - 4.0))
        q = r * r
        scale = (2.0 / sigma_sq) * q / (alpha_reach * alpha_reach)
        table = np.stack([r, scale * (1 + q) / (1 - q) ** 3, scale / (1 - q) ** 2, np.log(r)])
        self.r_tables = [
            table[:, off : off + size]
            .reshape(4, space, g, length)
            .transpose(1, 0, 2, 3)
            .astype(np.float32)
            for off, size, g in zip(self.offs, self.chunks, self.groups)
        ]


def split(value):
    high = value.astype(jnp.bfloat16)
    low = (value - high.astype(jnp.float32)).astype(jnp.bfloat16)
    return high, low


def whole(shape):
    return pl.BlockSpec(shape, lambda at, place: (0,) * len(shape))


def call_once(kernel, name, out_shape, place, mine, args, scratch=()):
    at_space = place.shape[0] - 2
    picked = [
        pl.BlockSpec(
            (1, *m.shape[1:]),
            lambda at, place, n=m.ndim: (place[at_space],) + (0,) * (n - 1),
        )
        for m in mine
    ]
    return pl.pallas_call(
        kernel,
        out_shape=out_shape,
        grid_spec=pltpu.PrefetchScalarGridSpec(
            num_scalar_prefetch=1,
            grid=(1,),
            in_specs=picked + [whole(a.shape) for a in args],
            out_specs=jax.tree.map(lambda o: whole(o.shape), out_shape),
            scratch_shapes=scratch,
        ),
        compiler_params=params(),
        name=name,
    )(place, *[jnp.asarray(m) for m in mine], *args)


def params(**kw):
    return pltpu.CompilerParams(vmem_limit_bytes=vmem_bytes, **kw)


def force_kernel(plan, step_x, place_ref, warped, images, jac, d_ref, t_ref, *rest):
    outs, field = rest[:-1], rest[-1]
    n = len(plan.chunks)
    way, at = pl.program_id(0), pl.program_id(1)
    yh = plan.yl // 2
    count = warped.shape[0]
    length = plan.length
    rows = step_x * yh

    total = None
    for b in range(count):
        w = warped[b].reshape(rows, length)
        slope = jnp.dot(w, d_ref[...], preferred_element_type=jnp.float32)
        diff = images[b].reshape(rows, length).astype(jnp.float32) - w.astype(jnp.float32)
        term = jac[b].reshape(rows, length).astype(jnp.float32) * diff * slope
        total = term if total is None else total + term
    start = pl.multiple_of(at * rows, rows)
    for h in range(length // lane):
        field[h, pl.ds(start, rows), :] = total[:, h * lane : (h + 1) * lane]

    def transform(refs):
        per = max(1, 256 // plan.xl)
        for y0 in range(0, yh, per):
            lines = jnp.concatenate(
                [
                    jnp.concatenate(
                        [
                            field[h, pl.ds(y, plan.xl, stride=yh), :]
                            for h in range(length // lane)
                        ],
                        axis=1,
                    )
                    for y in range(y0, y0 + per)
                ],
                axis=0,
            )
            high, low = split(lines)
            both = jnp.concatenate([high, low, high], axis=1)
            out = lax.dot_general(
                t_ref[0], both, (((1,), (1,)), ((), ())), preferred_element_type=jnp.float32
            )
            for ref, off, size in zip(refs, plan.offs, plan.chunks):
                ref[:, y0 * plan.xl : (y0 + per) * plan.xl] = out[off : off + size]

    last = at == pl.num_programs(1) - 1

    @pl.when(jnp.logical_and(last, way == 0))
    def _():
        transform(outs[:n])

    @pl.when(jnp.logical_and(last, way == 1))
    def _():
        transform(outs[n:])


def force_blocks(plan, k, place, warped, images, jac):
    count, xl, _, length = warped.shape
    yh = plan.yl // 2
    step_x = xl
    source = pl.BlockSpec(
        (count, step_x, yh, length), lambda way, at, place: (0, at, 2 * place[2 * k + way] + way, 0)
    )
    shapes = [jax.ShapeDtypeStruct((c, plan.half), jnp.float32) for c in plan.chunks] * 2
    outs = pl.pallas_call(
        functools.partial(force_kernel, plan, step_x),
        out_shape=shapes,
        grid_spec=pltpu.PrefetchScalarGridSpec(
            num_scalar_prefetch=1,
            grid=(2, xl // step_x),
            in_specs=[
                source,
                source,
                source,
                pl.BlockSpec((length, length), lambda way, at, place: (0, 0)),
                pl.BlockSpec((1, length, 3 * length), lambda way, at, place: (place[plan.at_space], 0, 0)),
            ],
            out_specs=[pl.BlockSpec(s.shape, lambda way, at, place: (0, 0)) for s in shapes],
            scratch_shapes=[pltpu.VMEM((length // lane, xl * yh, lane), jnp.float32)],
        ),
        compiler_params=params(),
        cost_estimate=pl.CostEstimate(
            flops=16 * xl * yh * length * length,
            bytes_accessed=12 * count * xl * yh * length + 8 * xl * yh * length,
            transcendentals=0,
        ),
        name="force",
    )(place, warped, images, jac, jnp.asarray(plan.d_table), jnp.asarray(plan.t_table))
    n = len(plan.chunks)
    return outs[:n], outs[n:]


def join_kernel(plan, g, place_ref, right, right_local, left, left_local, *outs):
    for d, out in enumerate(outs):
        rows = slice(d * g, (d + 1) * g)
        out[:, : plan.half] = right[rows] + right_local[rows]
        out[:, plan.half :] = left[rows] + left_local[rows]


def join(plan, g, place, right, right_local, left, left_local):
    return call_once(
        functools.partial(join_kernel, plan, g),
        "join",
        [jax.ShapeDtypeStruct((g, plan.lanes), jnp.float32)] * plan.space,
        place,
        [],
        [right, right_local, left, left_local],
    )


def forward_kernel(plan, g, place_ref, r_ref, w_ref, *rest):
    pieces, f_ref, ends_ref = rest[: plan.space], rest[-2], rest[-1]
    me = place_ref[plan.at_space]
    total = None
    for d, piece in enumerate(pieces):
        lines = jnp.concatenate(
            [piece[:, t * lane : (t + 1) * lane] for t in range(plan.tiles)], axis=0
        )
        high, low = split(lines)
        both = jnp.concatenate([high, low, high], axis=1)
        term = jnp.dot(both, w_ref[me ^ d], preferred_element_type=jnp.float32)
        total = term if total is None else total + term
    f_ref[...] = total
    r = r_ref[0, 0]
    length = plan.length

    def line(y):
        t, a = y // plan.ty, y % plan.ty
        return f_ref[t * g : (t + 1) * g, a * length : (a + 1) * length]

    zero = jnp.zeros_like(r)
    v, w = zero, zero
    for y in range(plan.yl):
        w = r * (w + v)
        v = line(y) + r * v
    ends_ref[:, :length], ends_ref[:, length : 2 * length] = v, w
    v, w = zero, zero
    for y in range(plan.yl - 1, -1, -1):
        v = v + line(y)
        w = r * (w + v)
        v = r * v
    ends_ref[:, 2 * length : 3 * length], ends_ref[:, 3 * length :] = v, w


def forward_lines(plan, c, place, pieces):
    g = plan.groups[c]
    return call_once(
        functools.partial(forward_kernel, plan, g),
        "first_forward",
        [
            jax.ShapeDtypeStruct((plan.tiles * g, plan.ty * plan.length), jnp.float32),
            jax.ShapeDtypeStruct((g, 4 * plan.length), jnp.float32),
        ],
        place,
        [plan.r_tables[c]],
        [jnp.asarray(plan.w_table), *pieces],
    )


def backward_kernel(plan, g, place_ref, r_ref, v_ref, f_ref, *rest):
    ends_refs, outs, u_ref = rest[: plan.subj], rest[plan.subj : -1], rest[-1]
    me, block = place_ref[plan.at_space], place_ref[plan.at_subj]
    length = plan.length
    r, alpha, beta, log_r = (r_ref[0, i] for i in range(4))
    full = jnp.exp(float(length) * log_r)
    once = 1.0 / (1.0 - full)
    again = float(length) * full * once
    zero = jnp.zeros_like(r)
    carry = [zero] * 4
    for h, ref in enumerate(ends_refs):
        source = block if h == 0 else place_ref[h - 1]
        for i in (0, 2):
            between = block - 1 - source if i == 0 else source - 1 - block
            between = jnp.where(between < 0, between + plan.subj, between)
            reach = (between * plan.yl).astype(jnp.float32)
            power = once * jnp.exp(reach * log_r)
            v = ref[:g, i * length : (i + 1) * length]
            w = ref[:g, (i + 1) * length : (i + 2) * length]
            carry[i] = carry[i] + power * v
            carry[i + 1] = carry[i + 1] + power * (w + (reach + again) * v)

    def line(y):
        t, a = y // plan.ty, y % plan.ty
        return (slice(t * g, (t + 1) * g), slice(a * length, (a + 1) * length))

    v, w = carry[0], carry[1]
    for y in range(plan.yl):
        w = r * (w + v)
        v = f_ref[line(y)] + r * v
        u_ref[line(y)] = alpha * v + beta * w
    v, w = carry[2], carry[3]
    for y in range(plan.yl - 1, -1, -1):
        u_ref[line(y)] = u_ref[line(y)] + (alpha * v + beta * w)
        v = v + f_ref[line(y)]
        w = r * (w + v)
        v = r * v
    high, low = split(u_ref[...])
    both = jnp.concatenate([high, low, high], axis=1)
    for d, out in enumerate(outs):
        back = jnp.dot(both, v_ref[me ^ d], preferred_element_type=jnp.float32)
        for t in range(plan.tiles):
            out[:, t * lane : (t + 1) * lane] = back[t * g : (t + 1) * g]


def backward_lines(plan, c, place, f, ends):
    g = plan.groups[c]
    return call_once(
        functools.partial(backward_kernel, plan, g),
        "second_and_back",
        [jax.ShapeDtypeStruct((g, plan.lanes), jnp.float32)] * plan.space,
        place,
        [plan.r_tables[c]],
        [jnp.asarray(plan.v_table), f, *ends],
        scratch=[pltpu.VMEM(f.shape, jnp.float32)],
    )


def finish_kernel(plan, y_step, fresh, place_ref, high_ref, low_ref, base, *rest):
    pieces, out, field = rest[:-2], rest[-2], rest[-1]
    length, xl = plan.length, plan.xl
    table = jnp.concatenate([high_ref[0], high_ref[0], low_ref[0]], axis=0)
    for t in range(y_step // plan.ty):
        columns = jnp.concatenate([p[:, t * lane : (t + 1) * lane] for p in pieces], axis=0)
        high, low = split(columns.T)
        both = jnp.concatenate([high, low, high], axis=1)
        lines = jnp.dot(both, table, preferred_element_type=jnp.float32)
        for a in range(plan.ty):
            y = t * plan.ty + a
            for h in range(length // lane):
                field[h, pl.ds(y, xl, stride=y_step), :] = lines[
                    a * xl : (a + 1) * xl, h * lane : (h + 1) * lane
                ]
    for h in range(length // lane):
        cols = slice(h * lane, (h + 1) * lane)
        old = base[:, :, cols]
        if fresh:
            old = old - (2.0 * step_size) * old
        out[:, :, cols] = old + step_size * field[h].reshape(xl, y_step, lane)


def finish(plan, cs, place, base, fresh, pieces):
    xl, yl, length = base.shape
    y_step = 8
    width = y_step * xl
    rows = slice(plan.offs[cs[0]], plan.offs[cs[-1]] + plan.chunks[cs[-1]])
    high, low = (jnp.asarray(plan.i_table[:, i, rows]) for i in range(2))
    count = high.shape[1]
    table = pl.BlockSpec((1, count, length), lambda at, place: (place[plan.at_space], 0, 0))
    block = pl.BlockSpec((xl, y_step, length), lambda at, place: (0, at, 0))
    return pl.pallas_call(
        functools.partial(finish_kernel, plan, y_step, fresh),
        out_shape=jax.ShapeDtypeStruct(base.shape, jnp.float32),
        grid_spec=pltpu.PrefetchScalarGridSpec(
            num_scalar_prefetch=1,
            grid=(yl // y_step,),
            in_specs=[table, table, block]
            + [pl.BlockSpec((p.shape[0], width), lambda at, place: (0, at)) for p in pieces],
            out_specs=block,
            scratch_shapes=[pltpu.VMEM((length // lane, xl * y_step, lane), jnp.float32)],
        ),
        compiler_params=params(),
        name="last_back",
    )(place, high, low, base, *pieces)


def tie(first, second):
    return lax.optimization_barrier((first, second))


def over_space(plan, pieces):
    moved = [
        lax.ppermute(pieces[d], "space", [(i, i ^ d) for i in range(plan.space)])
        for d in range(1, plan.space)
    ]
    return [pieces[0], *moved]


def ring_body(plan, template_warped, subject_images, jacobians, velocity):
    subj = plan.subj
    j, s = lax.axis_index("subj"), lax.axis_index("space")
    table = plan.place_table
    place = lax.dynamic_slice(jnp.asarray(table), (j, s, 0), (1, 1, table.shape[2])).reshape(-1)
    to_right = [(plan.ring[i], plan.ring[(i + 1) % subj]) for i in range(subj)]
    to_left = [(b, a) for a, b in to_right]

    local = [
        force_blocks(plan, k, place, template_warped, subject_images, jacobians)
        for k in range(subj)
    ]

    def ring(c, beside):
        size = plan.chunks[c]
        right, left, extra = local[0][0][c], local[0][1][c], ()
        for k in range(1, subj):
            (right, left), extra = beside(k, (right, left))
            if extra:
                right = jnp.concatenate([right, extra[0]])
                left = jnp.concatenate([left, extra[1]])
            right = lax.ppermute(right, "subj", to_right)
            left = lax.ppermute(left, "subj", to_left)
            if extra:
                arrived.append((right[size:], left[size:]))
            if k < subj - 1:
                right = right[:size] + local[k][0][c]
                left = left[:size] + local[k][1][c]
        return join(
            plan, plan.groups[c], place, right, local[-1][0][c], left, local[-1][1][c]
        )

    def more_hops(own):
        right, left = arrived[-1] if arrived else (own, own)
        while len(arrived) < subj // 2:
            right = lax.ppermute(right, "subj", to_right)
            if len(arrived) < subj // 2 - 1:
                left = lax.ppermute(left, "subj", to_left)
            arrived.append((right, left))
        flat = [own] + [e for pair in arrived for e in pair]
        return flat[:subj]

    count = len(plan.chunks)
    base, fresh = velocity, True
    waiting = None
    pieces = None
    for c in range(count):
        arrived = []
        held = {}

        def beside(k, both):
            if c == 0:
                return both, ()
            if k == 1:
                both, held["own"] = tie(both, pieces[0])
                moved = over_space(plan, [held["own"], *pieces[1:]])[1:]
                held["near"], held["far"] = moved[:-1], moved[-1:]
            if k == near_step:
                both, held["near"] = tie(both, held["near"])
            if k == far_step:
                both, held["far"] = tie(both, held["far"])
                all_pieces = [held["own"], *held["near"], *held["far"]]
                held["lines"] = forward_lines(plan, c - 1, place, all_pieces)
            if k == ends_step:
                both, held["lines"] = tie(both, held["lines"])
            if k < ends_step or len(arrived) >= subj // 2:
                return both, ()
            own = held["lines"][1]
            return both, (arrived[-1] if arrived else (own, own))

        new_pieces = ring(c, beside)
        if c > 0:
            f, own = held["lines"]
            new_own, f = tie(new_pieces[0], f)
            new_pieces = [new_own, *new_pieces[1:]]
            back = backward_lines(plan, c - 1, place, f, more_hops(own))
            finished = over_space(plan, back)
            if c < count - 1:
                base, fresh = finish(plan, [c - 1], place, base, fresh, finished), False
        pieces = new_pieces
    arrived = []
    f, own = forward_lines(plan, count - 1, place, over_space(plan, pieces))
    ends = more_hops(own)
    if count > 1:
        f, finished = tie(f, finished)
        base, fresh = finish(plan, [count - 2], place, base, fresh, finished), False
    back = backward_lines(plan, count - 1, place, f, ends)
    return finish(plan, [count - 1], place, base, fresh, over_space(plan, back))


def smoothing_symbol(first, second, third, length):
    def damping(freq):
        turns = (freq % length).astype(jnp.float32)
        return 2.0 - 2.0 * jnp.cos(turns * (2.0 * math.pi / length))

    total = damping(first) + damping(second) + damping(third)
    return 1.0 / (1.0 + alpha_reach * total) ** 2


def transposing_body(template_warped, subject_images, jacobians, velocity):
    length = template_warped.shape[3]
    half = length // 2
    warped = template_warped.astype(jnp.float32)
    slope = (jnp.roll(warped, -1, axis=3) - jnp.roll(warped, 1, axis=3)) * 0.5
    partial_value = jnp.sum(
        jacobians.astype(jnp.float32) * (subject_images.astype(jnp.float32) - warped) * slope,
        axis=0,
    )
    forward, inverse, _ = packed_np(length)
    forward, inverse = forward.astype(np.float32), inverse.astype(np.float32)
    packed = jnp.einsum("xyz,zp->xpy", partial_value, forward, precision=highest)
    packed = lax.psum_scatter(packed, "subj", scatter_dimension=1, tiled=True)
    packed = packed * (2.0 / sigma_sq)
    spectra = jnp.einsum("xpy,yk->kpx", packed, forward, precision=highest)
    lines = lax.all_to_all(spectra, "space", split_axis=0, concat_axis=2, tiled=True)
    freq_lines = jnp.einsum("kpx,xw->kpw", lines, forward, precision=highest)

    def true_freq(index):
        return jnp.where(index <= half, index, index - half)

    def mine(axis, size):
        return true_freq(lax.axis_index(axis) * size + jnp.arange(size, dtype=jnp.int32))

    symbol = smoothing_symbol(
        mine("space", lines.shape[0])[:, None, None],
        mine("subj", lines.shape[1])[None, :, None],
        true_freq(jnp.arange(length, dtype=jnp.int32))[None, None, :],
        length,
    )
    back_lines = jnp.einsum("kpw,wx->xpk", freq_lines * symbol, inverse, precision=highest)
    columns = lax.all_to_all(back_lines, "space", split_axis=0, concat_axis=2, tiled=True)
    real_field = jnp.einsum("xpk,ky->xpy", columns, inverse, precision=highest)
    depth_lines = lax.all_to_all(real_field, "subj", split_axis=2, concat_axis=1, tiled=True)
    smoothed = jnp.einsum("xpy,pz->xyz", depth_lines, inverse, precision=highest)
    return velocity - step_size * (2.0 * velocity - smoothed)


def body(subj, space, template_warped, subject_images, jacobians, velocity):
    _, xl, _, length = template_warped.shape
    yl = velocity.shape[1]
    power_of_two = subj & (subj - 1) == 0 and space & (space - 1) == 0
    fits = (
        subj > 1
        and power_of_two
        and length % lane == 0
        and yl % 32 == 0
        and xl >= 16
        and lane % xl == 0
        and length // 8 // space % 8 == 0
        and yl * xl == 8 * length
    )
    if not fits:
        return transposing_body(template_warped, subject_images, jacobians, velocity)
    plan = Plan(length, xl, subj, space)
    return ring_body(plan, template_warped, subject_images, jacobians, velocity)


def solution(mesh):
    return jax.shard_map(
        functools.partial(body, mesh.shape["subj"], mesh.shape["space"]),
        mesh=mesh,
        in_specs=(
            P("subj", "space", None, None),
            P("subj", "space", None, None),
            P("subj", "space", None, None),
            P("space", "subj", None),
        ),
        out_specs=P("space", "subj", None),
        check_vma=False,
    )
```

```python
import functools
import math

import jax
import jax.numpy as jnp
import ml_dtypes
import numpy as np
from jax import lax
from jax.experimental import pallas as pl
from jax.experimental.pallas import tpu as pltpu
from jax.sharding import PartitionSpec as P

sigma_sq = 0.05
step_size = 0.25
alpha_reach = 16.0
highest = lax.Precision.HIGHEST
vmem_bytes = 50 * 1024 * 1024
lane = 128
early_eighths = 6
near_step, far_step, ends_step = 3, 4, 5


def split_bf16(table):
    high = table.astype(ml_dtypes.bfloat16)
    low = (table - high.astype(np.float64)).astype(ml_dtypes.bfloat16)
    return high, low


def packed_np(length):
    half = length // 2
    index = np.arange(length)
    freq = np.where(index <= half, index, index - half)
    angle = (index[:, None] * freq[None, :] % length) * (2.0 * math.pi / length)
    forward = np.where(index[None, :] <= half, np.cos(angle), np.sin(angle))
    weight = np.where((index == 0) | (index == half), 1.0, 2.0) / length
    lam = 2.0 - 2.0 * np.cos(freq * (2.0 * math.pi / length))
    return forward, (forward * weight[None, :]).T, lam


class Plan:
    def __init__(self, length, rows_x, subj, space):
        self.length, self.xl, self.subj, self.space = length, rows_x, subj, space
        self.yl = length // subj
        self.lanes = self.yl * self.xl
        self.half = self.lanes // 2
        self.ty = lane // self.xl if self.xl < lane else 1
        self.tiles = self.lanes // lane
        early = length * early_eighths // 8
        self.early, self.late = early, length - early
        self.chunks = [self.early, self.late]
        self.offs = [0, early]
        self.g, self.gl = self.early // space, self.late // subj
        ring = list(range(0, subj, 2)) + list(range(subj - 1, 0, -2))
        self.ring = ring
        rows = np.zeros((subj, space, 2 * subj + 2), np.int32)
        for at, j in enumerate(ring):
            for k in range(subj):
                rows[j, :, 2 * k] = ring[(at - 1 - k) % subj]
                rows[j, :, 2 * k + 1] = ring[(at + 1 + k) % subj]
            rows[j, :, 2 * subj] = np.arange(space)
            rows[j, :, 2 * subj + 1] = j
        self.place_table = rows
        self.at_space, self.at_subj = 2 * subj, 2 * subj + 1
        forward, inverse, lam = packed_np(length)
        high, low = split_bf16(forward.T)
        self.t_table = np.concatenate([high, high, low], axis=1)
        high, low = split_bf16(inverse)
        self.i_table = np.stack([high, low])
        lines = length // self.ty
        high, low = split_bf16(forward.reshape(lines, self.ty * length))
        self.y_table = np.concatenate([high, high, low], axis=0)
        wide = inverse.T.reshape(lines, self.ty, length).transpose(1, 0, 2)
        high, low = split_bf16(wide.reshape(length, length))
        self.g_table = np.concatenate([high, high, low], axis=1)
        eye = np.eye(self.ty)
        blocks = forward.reshape(space, self.xl, length)
        wide = np.einsum("ab,sxw->saxbw", eye, blocks).reshape(space, lane, self.ty * length)
        high, low = split_bf16(wide)
        self.w_table = np.concatenate([high, high, low], axis=1)
        blocks = inverse.reshape(length, space, self.xl)
        wide = np.einsum("ab,wsx->sawbx", eye, blocks).reshape(space, self.ty * length, lane)
        high, low = split_bf16(wide)
        self.v_table = np.concatenate([high, high, low], axis=1)
        index = np.arange(length)
        slope = np.zeros((length, length))
        slope[(index + 1) % length, index] += 0.5
        slope[(index - 1) % length, index] -= 0.5
        slope = slope.astype(ml_dtypes.bfloat16)
        self.d_table = np.concatenate([slope, self.t_table], axis=1)
        centre = (1.0 + alpha_reach * (lam[:, None] + lam[None, :])) / alpha_reach + 2.0
        r = 2.0 / (centre + np.sqrt(centre * centre - 4.0))
        q = r * r
        scale = (2.0 / sigma_sq) * q / (alpha_reach * alpha_reach)
        table = np.stack([r, scale * (1 + q) / (1 - q) ** 3, scale / (1 - q) ** 2, np.log(r)])
        table = table.astype(np.float32)
        early_rows = table[:, :early].reshape(4, space, self.g, length)
        self.r_early = early_rows.transpose(1, 0, 2, 3)
        late_rows = table[:, early:].reshape(4, subj, self.gl, length)
        self.r_late = late_rows.transpose(1, 0, 2, 3)


def split(value):
    high = value.astype(jnp.bfloat16)
    low = (value - high.astype(jnp.float32)).astype(jnp.bfloat16)
    return high, low


def call_once(kernel, name, out_shape, place, args, scratch=()):
    vmem = pl.BlockSpec(memory_space=pltpu.VMEM)
    return pl.pallas_call(
        kernel,
        out_shape=out_shape,
        in_specs=[pl.BlockSpec(memory_space=pltpu.SMEM)] + [vmem] * len(args),
        out_specs=jax.tree.map(lambda _: vmem, out_shape),
        scratch_shapes=scratch,
        compiler_params=params(),
        name=name,
    )(place, *[jnp.asarray(a) for a in args])


def params(**kw):
    return pltpu.CompilerParams(vmem_limit_bytes=vmem_bytes, **kw)


def force_kernel(plan, place_ref, warped, images, jac, table, *rest):
    outs, field = rest[:-1], rest[-1]
    me = place_ref[plan.at_space]
    n = len(plan.chunks)
    way = pl.program_id(0)
    yh = plan.yl // 2
    count = warped.shape[0]
    length = plan.length
    rows = plan.xl * yh

    total = None
    for b in range(count):
        w = warped[b].reshape(rows, length)
        slope = jnp.dot(w, table[:, :length], preferred_element_type=jnp.float32)
        diff = images[b].reshape(rows, length).astype(jnp.float32) - w.astype(jnp.float32)
        term = jac[b].reshape(rows, length).astype(jnp.float32) * diff * slope
        total = term if total is None else total + term
    field[...] = jnp.swapaxes(total.reshape(plan.xl, yh, length), 0, 1)

    def transform(refs):
        per = max(1, 256 // plan.xl)
        for y0 in range(0, yh, per):
            lines = field[y0 : y0 + per].reshape(per * plan.xl, length)
            high, low = split(lines)
            both = jnp.concatenate([high, low, high], axis=1)
            out = lax.dot_general(
                table[:, length:], both, (((1,), (1,)), ((), ())), preferred_element_type=jnp.float32
            )
            cols = slice(y0 * plan.xl, (y0 + per) * plan.xl)
            for d in range(plan.space):
                rows = pl.ds(pl.multiple_of((me ^ d) * plan.g, 8), plan.g)
                refs[0][rows, cols] = out[d * plan.g : (d + 1) * plan.g]
            refs[1][:, cols] = out[plan.early :]

    @pl.when(way == 0)
    def _():
        transform(outs[:n])

    @pl.when(way == 1)
    def _():
        transform(outs[n:])


def force_blocks(plan, k, place, warped, images, jac):
    count, xl, _, length = warped.shape
    yh = plan.yl // 2
    source = pl.BlockSpec(
        (count, xl, yh, length), lambda way, place: (0, 0, 2 * place[2 * k + way] + way, 0)
    )
    shapes = [jax.ShapeDtypeStruct((c, plan.half), jnp.float32) for c in plan.chunks] * 2
    outs = pl.pallas_call(
        functools.partial(force_kernel, plan),
        out_shape=shapes,
        grid_spec=pltpu.PrefetchScalarGridSpec(
            num_scalar_prefetch=1,
            grid=(2,),
            in_specs=[
                source,
                source,
                source,
                pl.BlockSpec((length, 4 * length), lambda way, place: (0, 0)),
            ],
            out_specs=[pl.BlockSpec(s.shape, lambda way, place: (0, 0)) for s in shapes],
            scratch_shapes=[pltpu.VMEM((yh, xl, length), jnp.float32)],
        ),
        compiler_params=params(),
        cost_estimate=pl.CostEstimate(
            flops=16 * xl * yh * length * length,
            bytes_accessed=12 * count * xl * yh * length + 8 * xl * yh * length,
            transcendentals=0,
        ),
        name="force",
    )(place, warped, images, jac, jnp.asarray(plan.d_table))
    n = len(plan.chunks)
    return outs[:n], outs[n:]


def join_kernel(plan, place_ref, right_local, left_local, right, left, *outs):
    for d, out in enumerate(outs):
        rows = slice(d * plan.g, (d + 1) * plan.g)
        out[:, : plan.half] = right[rows] + right_local[rows]
        out[:, plan.half :] = left[rows] + left_local[rows]


def join(plan, place, *args):
    return call_once(
        functools.partial(join_kernel, plan),
        "join",
        [jax.ShapeDtypeStruct((plan.g, plan.lanes), jnp.float32)] * plan.space,
        place,
        args,
    )


def regroup_kernel(plan, place_ref, *rest):
    sources, outs = rest[:-2], rest[-2:]
    for n, source in enumerate(sources):
        at = 2 * place_ref[n] + n % 2
        to = pl.ds(pl.multiple_of(at % plan.subj * plan.gl, 8), plan.gl)

        def put(way):
            for m in range(plan.subj):
                target = place_ref[2 * m + way]
                rows = pl.ds(pl.multiple_of(target * plan.gl, 8), plan.gl)
                outs[way][m, to, :] = source[rows, :]

        for way in range(2):
            pl.when(at // plan.subj == way)(functools.partial(put, way))


def regroup(plan, place, sources):
    shape = (plan.subj, plan.late, plan.half)
    return call_once(
        functools.partial(regroup_kernel, plan),
        "regroup",
        [jax.ShapeDtypeStruct(shape, jnp.float32)] * 2,
        place,
        sources,
    )


def forward_kernel(plan, place_ref, r_ref, w_ref, *rest):
    g = plan.g
    pieces, f_ref, ends_ref = rest[: plan.space], rest[-2], rest[-1]
    me = place_ref[plan.at_space]
    total = None
    for d, piece in enumerate(pieces):
        lines = jnp.concatenate(
            [piece[:, t * lane : (t + 1) * lane] for t in range(plan.tiles)], axis=0
        )
        high, low = split(lines)
        both = jnp.concatenate([high, low, high], axis=1)
        term = jnp.dot(both, w_ref[me ^ d], preferred_element_type=jnp.float32)
        total = term if total is None else total + term
    f_ref[...] = total
    r = r_ref[me, 0]
    length = plan.length

    def line(y):
        t, a = y // plan.ty, y % plan.ty
        return f_ref[t * g : (t + 1) * g, a * length : (a + 1) * length]

    zero = jnp.zeros_like(r)
    v, w = zero, zero
    for y in range(plan.yl):
        w = r * (w + v)
        v = line(y) + r * v
    ends_ref[:, :length], ends_ref[:, length : 2 * length] = v, w
    v, w = zero, zero
    for y in range(plan.yl - 1, -1, -1):
        v = v + line(y)
        w = r * (w + v)
        v = r * v
    ends_ref[:, 2 * length : 3 * length], ends_ref[:, 3 * length :] = v, w


def forward_lines(plan, place, pieces):
    return call_once(
        functools.partial(forward_kernel, plan),
        "first_forward",
        [
            jax.ShapeDtypeStruct((plan.tiles * plan.g, plan.ty * plan.length), jnp.float32),
            jax.ShapeDtypeStruct((plan.g, 4 * plan.length), jnp.float32),
        ],
        place,
        [plan.r_early, plan.w_table, *pieces],
    )


def enter(log_r, length, size, blocks, block, sources):
    full = jnp.exp(float(length) * log_r)
    once = 1.0 / (1.0 - full)
    again = float(length) * full * once
    carry = [jnp.zeros_like(log_r)] * 4
    g = log_r.shape[0]
    for source, ref in sources:
        for i in (0, 2):
            between = block - 1 - source if i == 0 else source - 1 - block
            between = jnp.where(between < 0, between + blocks, between)
            reach = (between * size).astype(jnp.float32)
            power = once * jnp.exp(reach * log_r)
            v = ref[:g, i * length : (i + 1) * length]
            w = ref[:g, (i + 1) * length : (i + 2) * length]
            carry[i] = carry[i] + power * v
            carry[i + 1] = carry[i + 1] + power * (w + (reach + again) * v)
    return carry


def backward_kernel(plan, place_ref, r_ref, v_ref, f_ref, *rest):
    ends_refs, outs, u_ref = rest[: plan.subj], rest[plan.subj : -1], rest[-1]
    me, block = place_ref[plan.at_space], place_ref[plan.at_subj]
    g, length = plan.g, plan.length
    r, alpha, beta, log_r = (r_ref[me, i] for i in range(4))
    sources = [(block if h == 0 else place_ref[h - 1], ref) for h, ref in enumerate(ends_refs)]
    carry = enter(log_r, length, plan.yl, plan.subj, block, sources)

    def line(y):
        t, a = y // plan.ty, y % plan.ty
        return (slice(t * g, (t + 1) * g), slice(a * length, (a + 1) * length))

    v, w = carry[0], carry[1]
    for y in range(plan.yl):
        w = r * (w + v)
        v = f_ref[line(y)] + r * v
        u_ref[line(y)] = alpha * v + beta * w
    v, w = carry[2], carry[3]
    for y in range(plan.yl - 1, -1, -1):
        u_ref[line(y)] = u_ref[line(y)] + (alpha * v + beta * w)
        v = v + f_ref[line(y)]
        w = r * (w + v)
        v = r * v
    high, low = split(u_ref[...])
    both = jnp.concatenate([high, low, high], axis=1)
    top = plan.space // 2
    tables = jnp.concatenate([v_ref[me ^ d] for d in range(plan.space)], axis=1)
    all_back = jnp.dot(both, tables, preferred_element_type=jnp.float32)
    for d in range(plan.space):
        out = outs[min(d, top)]
        first = max(d - top, 0) * g
        back = all_back[:, d * lane : (d + 1) * lane]
        for t in range(plan.tiles):
            out[first : first + g, t * lane : (t + 1) * lane] = back[t * g : (t + 1) * g]


def backward_lines(plan, place, f, ends):
    top = plan.space // 2
    counts = [plan.g] * top + [plan.g * top]
    return call_once(
        functools.partial(backward_kernel, plan),
        "second_and_back",
        [jax.ShapeDtypeStruct((c, plan.lanes), jnp.float32) for c in counts],
        place,
        [plan.r_early, plan.v_table, f, *ends],
        scratch=[pltpu.VMEM(f.shape, jnp.float32)],
    )


def late_forward_kernel(plan, place_ref, r_ref, y_ref, *rest):
    *arrived, f_ref, ends_ref, z_ref = rest
    length, gl, xl, ty = plan.length, plan.gl, plan.xl, plan.ty
    lines = length // ty
    tiles = plan.half // lane
    for way in range(2):
        local, ref = arrived[way], arrived[2 + way]
        for b in range(plan.subj):
            rows = slice(b * gl, (b + 1) * gl)
            for t in range(tiles):
                cols = slice(t * lane, (t + 1) * lane)
                to = ((way * plan.subj + b) * tiles + t) * gl
                z_ref[to : to + gl, :] = ref[rows, cols] + local[0, rows, cols]
    turned = jnp.concatenate([z_ref[pl.ds(p, lines, stride=gl), :].T for p in range(gl)], axis=0)
    high, low = split(turned)
    both = jnp.concatenate([high, low, high], axis=1)
    out = jnp.dot(both, y_ref[...], preferred_element_type=jnp.float32)
    for p in range(gl):
        value = None
        for a in range(ty):
            rows = slice(p * lane + a * xl, p * lane + (a + 1) * xl)
            term = out[rows, a * length : (a + 1) * length]
            value = term if value is None else value + term
        for h in range(length // lane):
            f_ref[h, pl.ds(p, xl, stride=gl), :] = value[:, h * lane : (h + 1) * lane]
    r = r_ref[place_ref[plan.at_subj], 0]

    def line(x):
        rows = slice(x * gl, (x + 1) * gl)
        return jnp.concatenate([f_ref[h, rows, :] for h in range(length // lane)], axis=1)

    zero = jnp.zeros_like(r)
    v, w = zero, zero
    for x in range(xl):
        w = r * (w + v)
        v = line(x) + r * v
    ends_ref[:, :length], ends_ref[:, length : 2 * length] = v, w
    v, w = zero, zero
    for x in range(xl - 1, -1, -1):
        v = v + line(x)
        w = r * (w + v)
        v = r * v
    ends_ref[:, 2 * length : 3 * length], ends_ref[:, 3 * length :] = v, w


def late_forward(plan, place, *args):
    return call_once(
        functools.partial(late_forward_kernel, plan),
        "second_forward",
        [
            jax.ShapeDtypeStruct((plan.length // lane, plan.xl * plan.gl, lane), jnp.float32),
            jax.ShapeDtypeStruct((plan.gl, 4 * plan.length), jnp.float32),
        ],
        place,
        [plan.r_late, plan.y_table, *args],
        scratch=[pltpu.VMEM((plan.length // plan.ty * plan.gl, lane), jnp.float32)],
    )


def late_backward_kernel(plan, place_ref, r_ref, g_ref, f_ref, *rest):
    ends_refs = rest[: plan.space]
    out_ref, u_ref, y_ref = rest[plan.space :]
    me = place_ref[plan.at_space]
    length, gl, xl, ty = plan.length, plan.gl, plan.xl, plan.ty
    lines, halves = length // ty, length // lane
    r, alpha, beta, log_r = (r_ref[place_ref[plan.at_subj], i] for i in range(4))
    sources = [(me ^ d, ref) for d, ref in enumerate(ends_refs)]
    carry = enter(log_r, length, xl, plan.space, me, sources)

    def line(ref, x):
        rows = slice(x * gl, (x + 1) * gl)
        return jnp.concatenate([ref[h, rows, :] for h in range(halves)], axis=1)

    def keep(x, value):
        for h in range(halves):
            u_ref[h, x * gl : (x + 1) * gl, :] = value[:, h * lane : (h + 1) * lane]

    v, w = carry[0], carry[1]
    for x in range(xl):
        w = r * (w + v)
        v = line(f_ref, x) + r * v
        keep(x, alpha * v + beta * w)
    v, w = carry[2], carry[3]
    for x in range(xl - 1, -1, -1):
        keep(x, line(u_ref, x) + (alpha * v + beta * w))
        v = v + line(f_ref, x)
        w = r * (w + v)
        v = r * v
    rows = jnp.concatenate(
        [
            jnp.concatenate(
                [u_ref[h, pl.ds(p, xl, stride=gl), :] for h in range(halves)], axis=1
            )
            for p in range(gl)
        ],
        axis=0,
    )
    high, low = split(rows)
    both = jnp.concatenate([high, low, high], axis=1)
    out = lax.dot_general(
        g_ref[...], both, (((1,), (1,)), ((), ())), preferred_element_type=jnp.float32
    )
    place_of = lax.broadcasted_iota(jnp.int32, (lines, lane), 1) // xl
    for p in range(gl):
        tile, spot = p // ty, p % ty
        value = None
        for a in range(ty):
            part = out[a * lines : (a + 1) * lines, tile * lane : (tile + 1) * lane]
            if a != spot:
                part = pltpu.roll(part, (a - spot) % ty * xl, 1)
            value = part if value is None else jnp.where(place_of == a, part, value)
        y_ref[pl.ds(p, lines, stride=gl), :] = value
    for j in range(plan.subj):
        for t in range(plan.tiles):
            start = (j * plan.tiles + t) * gl
            out_ref[j, :, t * lane : (t + 1) * lane] = y_ref[start : start + gl, :]


def late_backward(plan, place, f, ends):
    return call_once(
        functools.partial(late_backward_kernel, plan),
        "first_and_back",
        jax.ShapeDtypeStruct((plan.subj, plan.gl, plan.lanes), jnp.float32),
        place,
        [plan.r_late, plan.g_table, f, *ends],
        scratch=[
            pltpu.VMEM(f.shape, jnp.float32),
            pltpu.VMEM((plan.length // plan.ty * plan.gl, lane), jnp.float32),
        ],
    )


def finish_kernel(plan, y_step, place_ref, i_ref, velocity, *rest):
    pieces, out = rest[:-1], rest[-1]
    length, xl = plan.length, plan.xl
    me = place_ref[plan.at_space]
    starts = [pl.multiple_of((me ^ d) * plan.g, 8) for d in range(plan.space)]
    high, low = (
        jnp.concatenate(
            [i_ref[i, pl.ds(start, plan.g), :] for start in starts] + [i_ref[i, plan.early :, :]],
            axis=0,
        )
        for i in range(2)
    )
    table = jnp.concatenate([high, high, low], axis=0)
    lines = []
    for t in range(y_step // plan.ty):
        columns = jnp.concatenate([p[:, t * lane : (t + 1) * lane] for p in pieces], axis=0)
        high, low = split(columns.T)
        both = jnp.concatenate([high, low, high], axis=1)
        lines.append(jnp.dot(both, table, preferred_element_type=jnp.float32))
        if len(lines) * plan.ty == 8:
            y = (t + 1) * plan.ty - 8
            block = jnp.concatenate(lines, axis=0).reshape(8, xl, length)
            smoothed = jnp.swapaxes(block, 0, 1)
            vel = velocity[:, y : y + 8, :]
            out[:, y : y + 8, :] = vel - step_size * (2.0 * vel - smoothed)
            lines = []


def finish(plan, place, velocity, pieces):
    xl, yl, length = velocity.shape
    y_step = 16
    width = y_step * xl
    block = pl.BlockSpec((xl, y_step, length), lambda at, place: (0, at, 0))
    return pl.pallas_call(
        functools.partial(finish_kernel, plan, y_step),
        out_shape=jax.ShapeDtypeStruct(velocity.shape, jnp.float32),
        grid_spec=pltpu.PrefetchScalarGridSpec(
            num_scalar_prefetch=1,
            grid=(yl // y_step,),
            in_specs=[
                pl.BlockSpec((2, length, length), lambda at, place: (0, 0, 0)),
                block,
            ]
            + [pl.BlockSpec((p.shape[0], width), lambda at, place: (0, at)) for p in pieces],
            out_specs=block,
        ),
        compiler_params=params(),
        name="last_back",
    )(place, jnp.asarray(plan.i_table), velocity, *pieces)


def tie(first, second):
    return lax.optimization_barrier((first, second))


def over_one(plan, part, d):
    if d == 0:
        return part
    return lax.ppermute(part, "space", [(i, i ^ d) for i in range(plan.space)])


def over_space(plan, pieces):
    return [over_one(plan, piece, d) for d, piece in enumerate(pieces)]


def ring_body(plan, template_warped, subject_images, jacobians, velocity):
    subj, space, half = plan.subj, plan.space, plan.subj // 2
    j, s = lax.axis_index("subj"), lax.axis_index("space")
    table = plan.place_table
    place = lax.dynamic_slice(jnp.asarray(table), (j, s, 0), (1, 1, table.shape[2])).reshape(-1)
    to_right = [(plan.ring[i], plan.ring[(i + 1) % subj]) for i in range(subj)]
    to_left = [(b, a) for a, b in to_right]

    def go_round(both):
        return lax.ppermute(both[0], "subj", to_right), lax.ppermute(both[1], "subj", to_left)

    local = [
        force_blocks(plan, k, place, template_warped, subject_images, jacobians)
        for k in range(subj)
    ]

    both = local[0][0][0], local[0][1][0]
    for k in range(1, subj):
        both = go_round(both)
        if k < subj - 1:
            both = tuple(b + local[k][way][0] for way, b in enumerate(both))
    pieces = join(plan, place, local[-1][0][0], local[-1][1][0], *both)
    late = regroup(plan, place, [local[k][way][1] for k in range(subj) for way in range(2)])

    top = space // 2
    both, own = tie((late[0][0], late[1][0]), pieces[0])
    pieces = [own, *pieces[1:]]
    far = lax.ppermute(
        jnp.concatenate(pieces[top:]), "space", [(i, i ^ top) for i in range(space)]
    )
    moved = over_space(plan, pieces[:top])
    arrived = []
    for k in range(1, subj):
        if k == near_step:
            both, moved = tie(both, moved)
        if k == far_step:
            both, far = tie(both, far)
            far = [far[d * plan.g : (d + 1) * plan.g] for d in range(top)]
            f, ends = forward_lines(plan, place, [*moved, *over_space(plan, far)])
        if k == ends_step:
            both, (f, ends) = tie(both, (f, ends))
        if k >= ends_step and len(arrived) < half:
            extra = arrived[-1] if arrived else (ends, ends)
            both = tuple(jnp.concatenate([b, e]) for b, e in zip(both, extra))
        both = go_round(both)
        if both[0].shape[0] > plan.late:
            arrived.append(tuple(b[plan.late :] for b in both))
        if k < subj - 1:
            both = tuple(b[: plan.late] + late[way][k] for way, b in enumerate(both))
    while len(arrived) < half:
        arrived.append(go_round(arrived[-1] if arrived else (ends, ends)))
    all_ends = [ends] + [e for pair in arrived for e in pair]

    f_late, ends_late = late_forward(
        plan, place, late[0][subj - 1 :], late[1][subj - 1 :], *both
    )
    others = [over_one(plan, ends_late, d) for d in range(space)]
    f, others = tie(f, others)
    *back, far = backward_lines(plan, place, f, all_ends[:subj])
    far = lax.ppermute(far, "space", [(i, i ^ top) for i in range(space)])
    back = over_space(plan, back)
    f_late, back = tie(f_late, back)
    back_late = late_backward(plan, place, f_late, others)
    back_late = lax.all_to_all(back_late, "subj", 0, 0)
    back_late = back_late.reshape(plan.late, plan.lanes)
    far = [far[d * plan.g : (d + 1) * plan.g] for d in range(top)]
    back += over_space(plan, far)
    return finish(plan, place, velocity, [*back, back_late])


def smoothing_symbol(first, second, third, length):
    def damping(freq):
        turns = (freq % length).astype(jnp.float32)
        return 2.0 - 2.0 * jnp.cos(turns * (2.0 * math.pi / length))

    total = damping(first) + damping(second) + damping(third)
    return 1.0 / (1.0 + alpha_reach * total) ** 2


def transposing_body(template_warped, subject_images, jacobians, velocity):
    length = template_warped.shape[3]
    half = length // 2
    warped = template_warped.astype(jnp.float32)
    slope = (jnp.roll(warped, -1, axis=3) - jnp.roll(warped, 1, axis=3)) * 0.5
    partial_value = jnp.sum(
        jacobians.astype(jnp.float32) * (subject_images.astype(jnp.float32) - warped) * slope,
        axis=0,
    )
    forward, inverse, _ = packed_np(length)
    forward, inverse = forward.astype(np.float32), inverse.astype(np.float32)
    packed = jnp.einsum("xyz,zp->xpy", partial_value, forward, precision=highest)
    packed = lax.psum_scatter(packed, "subj", scatter_dimension=1, tiled=True)
    packed = packed * (2.0 / sigma_sq)
    spectra = jnp.einsum("xpy,yk->kpx", packed, forward, precision=highest)
    lines = lax.all_to_all(spectra, "space", split_axis=0, concat_axis=2, tiled=True)
    freq_lines = jnp.einsum("kpx,xw->kpw", lines, forward, precision=highest)

    def true_freq(index):
        return jnp.where(index <= half, index, index - half)

    def mine(axis, size):
        return true_freq(lax.axis_index(axis) * size + jnp.arange(size, dtype=jnp.int32))

    symbol = smoothing_symbol(
        mine("space", lines.shape[0])[:, None, None],
        mine("subj", lines.shape[1])[None, :, None],
        true_freq(jnp.arange(length, dtype=jnp.int32))[None, None, :],
        length,
    )
    back_lines = jnp.einsum("kpw,wx->xpk", freq_lines * symbol, inverse, precision=highest)
    columns = lax.all_to_all(back_lines, "space", split_axis=0, concat_axis=2, tiled=True)
    real_field = jnp.einsum("xpk,ky->xpy", columns, inverse, precision=highest)
    depth_lines = lax.all_to_all(real_field, "subj", split_axis=2, concat_axis=1, tiled=True)
    smoothed = jnp.einsum("xpy,pz->xyz", depth_lines, inverse, precision=highest)
    return velocity - step_size * (2.0 * velocity - smoothed)


def body(subj, space, template_warped, subject_images, jacobians, velocity):
    _, xl, _, length = template_warped.shape
    yl = velocity.shape[1]
    power_of_two = subj & (subj - 1) == 0 and space & (space - 1) == 0
    fits = (
        subj > 1
        and power_of_two
        and length % lane == 0
        and yl % 32 == 0
        and xl >= 16
        and lane % xl == 0
        and 2 * xl == lane
        and early_eighths * length // 8 % (8 * space) == 0
        and (8 - early_eighths) * length // 8 % (8 * subj) == 0
        and yl * xl == 8 * length
    )
    if not fits:
        return transposing_body(template_warped, subject_images, jacobians, velocity)
    plan = Plan(length, xl, subj, space)
    return ring_body(plan, template_warped, subject_images, jacobians, velocity)


def solution(mesh):
    return jax.shard_map(
        functools.partial(body, mesh.shape["subj"], mesh.shape["space"]),
        mesh=mesh,
        in_specs=(
            P("subj", "space", None, None),
            P("subj", "space", None, None),
            P("subj", "space", None, None),
            P("space", "subj", None),
        ),
        out_specs=P("space", "subj", None),
        check_vma=False,
    )
```

```python
import functools
import math

import jax
import jax.numpy as jnp
import ml_dtypes
import numpy as np
from jax import lax
from jax.experimental import pallas as pl
from jax.experimental.pallas import tpu as pltpu
from jax.sharding import PartitionSpec as P

sigma_sq = 0.05
step_size = 0.25
alpha_reach = 16.0
highest = lax.Precision.HIGHEST
vmem_bytes = 50 * 1024 * 1024
lane = 128
early_eighths = 6
early_parts = 2
near_step, far_step, ends_step = 3, 4, 5


def split_bf16(table):
    high = table.astype(ml_dtypes.bfloat16)
    low = (table - high.astype(np.float64)).astype(ml_dtypes.bfloat16)
    return high, low


def packed_np(length):
    half = length // 2
    index = np.arange(length)
    freq = np.where(index <= half, index, index - half)
    angle = (index[:, None] * freq[None, :] % length) * (2.0 * math.pi / length)
    forward = np.where(index[None, :] <= half, np.cos(angle), np.sin(angle))
    weight = np.where((index == 0) | (index == half), 1.0, 2.0) / length
    lam = 2.0 - 2.0 * np.cos(freq * (2.0 * math.pi / length))
    return forward, (forward * weight[None, :]).T, lam


class Plan:
    def __init__(self, length, rows_x, subj, space):
        self.length, self.xl, self.subj, self.space = length, rows_x, subj, space
        self.yl = length // subj
        self.lanes = self.yl * self.xl
        self.half = self.lanes // 2
        self.ty = lane // self.xl if self.xl < lane else 1
        self.tiles = self.lanes // lane
        early = length * early_eighths // 8
        self.early, self.late = early, length - early
        self.chunks = [self.early, self.late]
        self.part = early // early_parts
        self.g, self.gl = self.early // space, self.late // subj
        ring = list(range(0, subj, 2)) + list(range(subj - 1, 0, -2))
        self.ring = ring
        rows = np.zeros((subj, space, 2 * subj + 2), np.int32)
        for at, j in enumerate(ring):
            for k in range(subj):
                rows[j, :, 2 * k] = ring[(at - 1 - k) % subj]
                rows[j, :, 2 * k + 1] = ring[(at + 1 + k) % subj]
            rows[j, :, 2 * subj] = np.arange(space)
            rows[j, :, 2 * subj + 1] = j
        self.place_table = rows
        self.at_space, self.at_subj = 2 * subj, 2 * subj + 1
        forward, inverse, lam = packed_np(length)
        high, low = split_bf16(forward.T)
        self.t_table = np.concatenate([high, high, low], axis=1)
        high, low = split_bf16(inverse)
        self.i_table = np.stack([high, low])
        lines = length // self.ty
        high, low = split_bf16(forward.reshape(lines, self.ty * length))
        self.y_table = np.concatenate([high, high, low], axis=0)
        wide = inverse.T.reshape(lines, self.ty, length).transpose(1, 0, 2)
        high, low = split_bf16(wide.reshape(length, length))
        self.g_table = np.concatenate([high, high, low], axis=1)
        eye = np.eye(self.ty)
        blocks = forward.reshape(space, self.xl, length)
        wide = np.einsum("ab,sxw->saxbw", eye, blocks).reshape(space, lane, self.ty * length)
        high, low = split_bf16(wide)
        self.w_table = np.concatenate([high, high, low], axis=1)
        blocks = inverse.reshape(length, space, self.xl)
        wide = np.einsum("ab,wsx->sawbx", eye, blocks).reshape(space, self.ty * length, lane)
        high, low = split_bf16(wide)
        self.v_table = np.concatenate([high, high, low], axis=1)
        index = np.arange(length)
        slope = np.zeros((length, length))
        slope[(index + 1) % length, index] += 0.5
        slope[(index - 1) % length, index] -= 0.5
        slope = slope.astype(ml_dtypes.bfloat16)
        self.d_table = np.concatenate([slope, self.t_table], axis=1)
        centre = (1.0 + alpha_reach * (lam[:, None] + lam[None, :])) / alpha_reach + 2.0
        r = 2.0 / (centre + np.sqrt(centre * centre - 4.0))
        q = r * r
        scale = (2.0 / sigma_sq) * q / (alpha_reach * alpha_reach)
        table = np.stack([r, scale * (1 + q) / (1 - q) ** 3, scale / (1 - q) ** 2, np.log(r)])
        table = table.astype(np.float32)
        early_rows = table[:, :early].reshape(4, space, self.g, length)
        self.r_early = early_rows.transpose(1, 0, 2, 3)
        late_rows = table[:, early:].reshape(4, subj, self.gl, length)
        self.r_late = late_rows.transpose(1, 0, 2, 3)


def split(value):
    high = value.astype(jnp.bfloat16)
    low = (value - high.astype(jnp.float32)).astype(jnp.bfloat16)
    return high, low


def call_once(kernel, name, out_shape, place, args, scratch=()):
    vmem = pl.BlockSpec(memory_space=pltpu.VMEM)
    return pl.pallas_call(
        kernel,
        out_shape=out_shape,
        in_specs=[pl.BlockSpec(memory_space=pltpu.SMEM)] + [vmem] * len(args),
        out_specs=jax.tree.map(lambda _: vmem, out_shape),
        scratch_shapes=scratch,
        compiler_params=params(),
        name=name,
    )(place, *[jnp.asarray(a) for a in args])


def params(**kw):
    return pltpu.CompilerParams(vmem_limit_bytes=vmem_bytes, **kw)


def force_kernel(plan, place_ref, warped, images, jac, table, *rest):
    outs, field = rest[:-1], rest[-1]
    me = place_ref[plan.at_space]
    n = len(outs) // 2
    way = pl.program_id(0)
    yh = plan.yl // 2
    count = warped.shape[0]
    length = plan.length
    rows = plan.xl * yh

    total = None
    for b in range(count):
        w = warped[b].reshape(rows, length)
        slope = jnp.dot(w, table[:, :length], preferred_element_type=jnp.float32)
        diff = images[b].reshape(rows, length).astype(jnp.float32) - w.astype(jnp.float32)
        term = jac[b].reshape(rows, length).astype(jnp.float32) * diff * slope
        total = term if total is None else total + term
    field[...] = jnp.swapaxes(total.reshape(plan.xl, yh, length), 0, 1)

    def transform(refs):
        starts = [pl.multiple_of((me ^ d) * plan.g, 16) for d in range(plan.space)]
        rows_of = [table[pl.ds(start, plan.g), length:] for start in starts]
        ordered = jnp.concatenate([*rows_of, table[plan.early :, length:]], axis=0)
        per = max(1, 256 // plan.xl)
        for y0 in range(0, yh, per):
            lines = field[y0 : y0 + per].reshape(per * plan.xl, length)
            high, low = split(lines)
            both = jnp.concatenate([high, low, high], axis=1)
            out = lax.dot_general(
                ordered, both, (((1,), (1,)), ((), ())), preferred_element_type=jnp.float32
            )
            cols = slice(y0 * plan.xl, (y0 + per) * plan.xl)
            first = 0
            for ref in refs:
                ref[:, cols] = out[first : first + ref.shape[0]]
                first += ref.shape[0]

    @pl.when(way == 0)
    def _():
        transform(outs[:n])

    @pl.when(way == 1)
    def _():
        transform(outs[n:])


def force_blocks(plan, k, place, warped, images, jac):
    count, xl, _, length = warped.shape
    yh = plan.yl // 2
    source = pl.BlockSpec(
        (count, xl, yh, length), lambda way, place: (0, 0, 2 * place[2 * k + way] + way, 0)
    )
    sizes = [plan.part] * early_parts + [plan.late]
    shapes = [jax.ShapeDtypeStruct((c, plan.half), jnp.float32) for c in sizes] * 2
    outs = pl.pallas_call(
        functools.partial(force_kernel, plan),
        out_shape=shapes,
        grid_spec=pltpu.PrefetchScalarGridSpec(
            num_scalar_prefetch=1,
            grid=(2,),
            in_specs=[
                source,
                source,
                source,
                pl.BlockSpec((length, 4 * length), lambda way, place: (0, 0)),
            ],
            out_specs=[pl.BlockSpec(s.shape, lambda way, place: (0, 0)) for s in shapes],
            scratch_shapes=[pltpu.VMEM((yh, xl, length), jnp.float32)],
        ),
        compiler_params=params(),
        cost_estimate=pl.CostEstimate(
            flops=16 * xl * yh * length * length,
            bytes_accessed=12 * count * xl * yh * length + 8 * xl * yh * length,
            transcendentals=0,
        ),
        name="force",
    )(place, warped, images, jac, jnp.asarray(plan.d_table))
    n = len(sizes)
    return outs[:n], outs[n:]


def join_kernel(plan, place_ref, *rest):
    arrived, outs = rest[: -plan.space], rest[-plan.space :]
    per = plan.part // plan.g
    for d, out in enumerate(outs):
        part, at = d // per, d % per * plan.g
        for way in range(2):
            mine, came = arrived[(2 * part + way) * 2 : (2 * part + way) * 2 + 2]
            cols = slice(way * plan.half, (way + 1) * plan.half)
            out[:, cols] = mine[at : at + plan.g] + came[at : at + plan.g]


def join(plan, place, args):
    return call_once(
        functools.partial(join_kernel, plan),
        "join",
        [jax.ShapeDtypeStruct((plan.g, plan.lanes), jnp.float32)] * plan.space,
        place,
        args,
    )


def regroup_kernel(plan, place_ref, *rest):
    sources, outs = rest[:-2], rest[-2:]
    for n, source in enumerate(sources):
        at = 2 * place_ref[n] + n % 2
        to = pl.ds(pl.multiple_of(at % plan.subj * plan.gl, 8), plan.gl)

        def put(way):
            for m in range(plan.subj):
                target = place_ref[2 * m + way]
                rows = pl.ds(pl.multiple_of(target * plan.gl, 8), plan.gl)
                outs[way][m, to, :] = source[rows, :]

        for way in range(2):
            pl.when(at // plan.subj == way)(functools.partial(put, way))


def regroup(plan, place, sources):
    shape = (plan.subj, plan.late, plan.half)
    return call_once(
        functools.partial(regroup_kernel, plan),
        "regroup",
        [jax.ShapeDtypeStruct(shape, jnp.float32)] * 2,
        place,
        sources,
    )


def forward_kernel(plan, place_ref, r_ref, w_ref, *rest):
    g = plan.g
    pieces, f_ref, ends_ref = rest[: plan.space], rest[-2], rest[-1]
    me = place_ref[plan.at_space]
    total = None
    for d, piece in enumerate(pieces):
        lines = jnp.concatenate(
            [piece[:, t * lane : (t + 1) * lane] for t in range(plan.tiles)], axis=0
        )
        high, low = split(lines)
        both = jnp.concatenate([high, low, high], axis=1)
        term = jnp.dot(both, w_ref[me ^ d], preferred_element_type=jnp.float32)
        total = term if total is None else total + term
    f_ref[...] = total
    r = r_ref[me, 0]
    length = plan.length

    def line(y):
        t, a = y // plan.ty, y % plan.ty
        return f_ref[t * g : (t + 1) * g, a * length : (a + 1) * length]

    zero = jnp.zeros_like(r)
    v, w = zero, zero
    for y in range(plan.yl):
        w = r * (w + v)
        v = line(y) + r * v
    ends_ref[:, :length], ends_ref[:, length : 2 * length] = v, w
    v, w = zero, zero
    for y in range(plan.yl - 1, -1, -1):
        v = v + line(y)
        w = r * (w + v)
        v = r * v
    ends_ref[:, 2 * length : 3 * length], ends_ref[:, 3 * length :] = v, w


def forward_lines(plan, place, pieces):
    return call_once(
        functools.partial(forward_kernel, plan),
        "first_forward",
        [
            jax.ShapeDtypeStruct((plan.tiles * plan.g, plan.ty * plan.length), jnp.float32),
            jax.ShapeDtypeStruct((plan.g, 4 * plan.length), jnp.float32),
        ],
        place,
        [plan.r_early, plan.w_table, *pieces],
    )


def enter(log_r, length, size, blocks, block, sources):
    full = jnp.exp(float(length) * log_r)
    once = 1.0 / (1.0 - full)
    again = float(length) * full * once
    carry = [jnp.zeros_like(log_r)] * 4
    g = log_r.shape[0]
    for source, ref in sources:
        for i in (0, 2):
            between = block - 1 - source if i == 0 else source - 1 - block
            between = jnp.where(between < 0, between + blocks, between)
            reach = (between * size).astype(jnp.float32)
            power = once * jnp.exp(reach * log_r)
            v = ref[:g, i * length : (i + 1) * length]
            w = ref[:g, (i + 1) * length : (i + 2) * length]
            carry[i] = carry[i] + power * v
            carry[i + 1] = carry[i + 1] + power * (w + (reach + again) * v)
    return carry


def backward_kernel(plan, place_ref, r_ref, v_ref, f_ref, *rest):
    ends_refs, outs, u_ref = rest[: plan.subj], rest[plan.subj : -1], rest[-1]
    me, block = place_ref[plan.at_space], place_ref[plan.at_subj]
    g, length = plan.g, plan.length
    r, alpha, beta, log_r = (r_ref[me, i] for i in range(4))
    sources = [(block if h == 0 else place_ref[h - 1], ref) for h, ref in enumerate(ends_refs)]
    carry = enter(log_r, length, plan.yl, plan.subj, block, sources)

    def line(y):
        t, a = y // plan.ty, y % plan.ty
        return (slice(t * g, (t + 1) * g), slice(a * length, (a + 1) * length))

    v, w = carry[0], carry[1]
    for y in range(plan.yl):
        w = r * (w + v)
        v = f_ref[line(y)] + r * v
        u_ref[line(y)] = alpha * v + beta * w
    v, w = carry[2], carry[3]
    for y in range(plan.yl - 1, -1, -1):
        u_ref[line(y)] = u_ref[line(y)] + (alpha * v + beta * w)
        v = v + f_ref[line(y)]
        w = r * (w + v)
        v = r * v
    high, low = split(u_ref[...])
    both = jnp.concatenate([high, low, high], axis=1)
    top = plan.space // 2
    tables = jnp.concatenate([v_ref[me ^ d] for d in range(plan.space)], axis=1)
    all_back = jnp.dot(both, tables, preferred_element_type=jnp.float32)
    for d in range(plan.space):
        out = outs[min(d, top)]
        first = max(d - top, 0) * g
        back = all_back[:, d * lane : (d + 1) * lane]
        for t in range(plan.tiles):
            out[first : first + g, t * lane : (t + 1) * lane] = back[t * g : (t + 1) * g]


def backward_lines(plan, place, f, ends):
    top = plan.space // 2
    counts = [plan.g] * top + [plan.g * top]
    return call_once(
        functools.partial(backward_kernel, plan),
        "second_and_back",
        [jax.ShapeDtypeStruct((c, plan.lanes), jnp.float32) for c in counts],
        place,
        [plan.r_early, plan.v_table, f, *ends],
        scratch=[pltpu.VMEM(f.shape, jnp.float32)],
    )


def late_forward_kernel(plan, place_ref, r_ref, y_ref, *rest):
    *arrived, f_ref, ends_ref, z_ref = rest
    length, gl, xl, ty = plan.length, plan.gl, plan.xl, plan.ty
    lines = length // ty
    tiles = plan.half // lane
    for way in range(2):
        local, ref = arrived[way], arrived[2 + way]
        for b in range(plan.subj):
            rows = slice(b * gl, (b + 1) * gl)
            for t in range(tiles):
                cols = slice(t * lane, (t + 1) * lane)
                to = ((way * plan.subj + b) * tiles + t) * gl
                z_ref[to : to + gl, :] = ref[rows, cols] + local[0, rows, cols]
    turned = jnp.concatenate([z_ref[pl.ds(p, lines, stride=gl), :].T for p in range(gl)], axis=0)
    high, low = split(turned)
    both = jnp.concatenate([high, low, high], axis=1)
    out = jnp.dot(both, y_ref[...], preferred_element_type=jnp.float32)
    for p in range(gl):
        value = None
        for a in range(ty):
            rows = slice(p * lane + a * xl, p * lane + (a + 1) * xl)
            term = out[rows, a * length : (a + 1) * length]
            value = term if value is None else value + term
        for h in range(length // lane):
            f_ref[h, pl.ds(p, xl, stride=gl), :] = value[:, h * lane : (h + 1) * lane]
    r = r_ref[place_ref[plan.at_subj], 0]

    def line(x):
        rows = slice(x * gl, (x + 1) * gl)
        return jnp.concatenate([f_ref[h, rows, :] for h in range(length // lane)], axis=1)

    zero = jnp.zeros_like(r)
    v, w = zero, zero
    for x in range(xl):
        w = r * (w + v)
        v = line(x) + r * v
    ends_ref[:, :length], ends_ref[:, length : 2 * length] = v, w
    v, w = zero, zero
    for x in range(xl - 1, -1, -1):
        v = v + line(x)
        w = r * (w + v)
        v = r * v
    ends_ref[:, 2 * length : 3 * length], ends_ref[:, 3 * length :] = v, w


def late_forward(plan, place, *args):
    return call_once(
        functools.partial(late_forward_kernel, plan),
        "second_forward",
        [
            jax.ShapeDtypeStruct((plan.length // lane, plan.xl * plan.gl, lane), jnp.float32),
            jax.ShapeDtypeStruct((plan.gl, 4 * plan.length), jnp.float32),
        ],
        place,
        [plan.r_late, plan.y_table, *args],
        scratch=[pltpu.VMEM((plan.length // plan.ty * plan.gl, lane), jnp.float32)],
    )


def late_backward_kernel(plan, place_ref, r_ref, g_ref, f_ref, *rest):
    ends_refs = rest[: plan.space]
    out_ref, u_ref, y_ref = rest[plan.space :]
    me = place_ref[plan.at_space]
    length, gl, xl, ty = plan.length, plan.gl, plan.xl, plan.ty
    lines, halves = length // ty, length // lane
    r, alpha, beta, log_r = (r_ref[place_ref[plan.at_subj], i] for i in range(4))
    sources = [(me ^ d, ref) for d, ref in enumerate(ends_refs)]
    carry = enter(log_r, length, xl, plan.space, me, sources)

    def line(ref, x):
        rows = slice(x * gl, (x + 1) * gl)
        return jnp.concatenate([ref[h, rows, :] for h in range(halves)], axis=1)

    def keep(x, value):
        for h in range(halves):
            u_ref[h, x * gl : (x + 1) * gl, :] = value[:, h * lane : (h + 1) * lane]

    v, w = carry[0], carry[1]
    for x in range(xl):
        w = r * (w + v)
        v = line(f_ref, x) + r * v
        keep(x, alpha * v + beta * w)
    v, w = carry[2], carry[3]
    for x in range(xl - 1, -1, -1):
        keep(x, line(u_ref, x) + (alpha * v + beta * w))
        v = v + line(f_ref, x)
        w = r * (w + v)
        v = r * v
    rows = jnp.concatenate(
        [
            jnp.concatenate(
                [u_ref[h, pl.ds(p, xl, stride=gl), :] for h in range(halves)], axis=1
            )
            for p in range(gl)
        ],
        axis=0,
    )
    high, low = split(rows)
    both = jnp.concatenate([high, low, high], axis=1)
    out = lax.dot_general(
        g_ref[...], both, (((1,), (1,)), ((), ())), preferred_element_type=jnp.float32
    )
    place_of = lax.broadcasted_iota(jnp.int32, (lines, lane), 1) // xl
    for p in range(gl):
        tile, spot = p // ty, p % ty
        value = None
        for a in range(ty):
            part = out[a * lines : (a + 1) * lines, tile * lane : (tile + 1) * lane]
            if a != spot:
                part = pltpu.roll(part, (a - spot) % ty * xl, 1)
            value = part if value is None else jnp.where(place_of == a, part, value)
        y_ref[pl.ds(p, lines, stride=gl), :] = value
    for j in range(plan.subj):
        for t in range(plan.tiles):
            start = (j * plan.tiles + t) * gl
            out_ref[j, :, t * lane : (t + 1) * lane] = y_ref[start : start + gl, :]


def late_backward(plan, place, f, ends):
    return call_once(
        functools.partial(late_backward_kernel, plan),
        "first_and_back",
        jax.ShapeDtypeStruct((plan.subj, plan.gl, plan.lanes), jnp.float32),
        place,
        [plan.r_late, plan.g_table, f, *ends],
        scratch=[
            pltpu.VMEM(f.shape, jnp.float32),
            pltpu.VMEM((plan.length // plan.ty * plan.gl, lane), jnp.float32),
        ],
    )


def finish_kernel(plan, y_step, place_ref, i_ref, velocity, *rest):
    pieces, out = rest[:-1], rest[-1]
    length, xl = plan.length, plan.xl
    me = place_ref[plan.at_space]
    starts = [pl.multiple_of((me ^ d) * plan.g, 8) for d in range(plan.space)]
    high, low = (
        jnp.concatenate(
            [i_ref[i, pl.ds(start, plan.g), :] for start in starts] + [i_ref[i, plan.early :, :]],
            axis=0,
        )
        for i in range(2)
    )
    table = jnp.concatenate([high, high, low], axis=0)
    lines = []
    for t in range(y_step // plan.ty):
        columns = jnp.concatenate([p[:, t * lane : (t + 1) * lane] for p in pieces], axis=0)
        high, low = split(columns.T)
        both = jnp.concatenate([high, low, high], axis=1)
        lines.append(jnp.dot(both, table, preferred_element_type=jnp.float32))
        if len(lines) * plan.ty == 8:
            y = (t + 1) * plan.ty - 8
            block = jnp.concatenate(lines, axis=0).reshape(8, xl, length)
            smoothed = jnp.swapaxes(block, 0, 1)
            vel = velocity[:, y : y + 8, :]
            out[:, y : y + 8, :] = vel - step_size * (2.0 * vel - smoothed)
            lines = []


def finish(plan, place, velocity, pieces):
    xl, yl, length = velocity.shape
    y_step = 16
    width = y_step * xl
    block = pl.BlockSpec((xl, y_step, length), lambda at, place: (0, at, 0))
    return pl.pallas_call(
        functools.partial(finish_kernel, plan, y_step),
        out_shape=jax.ShapeDtypeStruct(velocity.shape, jnp.float32),
        grid_spec=pltpu.PrefetchScalarGridSpec(
            num_scalar_prefetch=1,
            grid=(yl // y_step,),
            in_specs=[
                pl.BlockSpec((2, length, length), lambda at, place: (0, 0, 0)),
                block,
            ]
            + [pl.BlockSpec((p.shape[0], width), lambda at, place: (0, at)) for p in pieces],
            out_specs=block,
        ),
        compiler_params=params(),
        name="last_back",
    )(place, jnp.asarray(plan.i_table), velocity, *pieces)


def tie(first, second):
    return lax.optimization_barrier((first, second))


def over_one(plan, part, d):
    if d == 0:
        return part
    return lax.ppermute(part, "space", [(i, i ^ d) for i in range(plan.space)])


def over_space(plan, pieces):
    return [over_one(plan, piece, d) for d, piece in enumerate(pieces)]


def ring_body(plan, template_warped, subject_images, jacobians, velocity):
    subj, space, half = plan.subj, plan.space, plan.subj // 2
    j, s = lax.axis_index("subj"), lax.axis_index("space")
    table = plan.place_table
    place = lax.dynamic_slice(jnp.asarray(table), (j, s, 0), (1, 1, table.shape[2])).reshape(-1)
    to_right = [(plan.ring[i], plan.ring[(i + 1) % subj]) for i in range(subj)]
    to_left = [(b, a) for a, b in to_right]

    def go_round(both):
        return lax.ppermute(both[0], "subj", to_right), lax.ppermute(both[1], "subj", to_left)

    local = [
        force_blocks(plan, k, place, template_warped, subject_images, jacobians)
        for k in range(subj)
    ]

    parts = range(early_parts)
    streams = [(local[0][0][p], local[0][1][p]) for p in parts]
    for k in range(1, subj):
        streams = [go_round(both) for both in streams]
        if k < subj - 1:
            streams = [
                tuple(b + local[k][way][p] for way, b in enumerate(both))
                for p, both in enumerate(streams)
            ]
    pieces = join(
        plan, place, [a for p in parts for way in range(2) for a in (local[-1][way][p], streams[p][way])]
    )
    late = regroup(plan, place, [local[k][way][-1] for k in range(subj) for way in range(2)])

    top = space // 2
    both, own = tie((late[0][0], late[1][0]), pieces[0])
    pieces = [own, *pieces[1:]]
    far = lax.ppermute(
        jnp.concatenate(pieces[top:]), "space", [(i, i ^ top) for i in range(space)]
    )
    moved = over_space(plan, pieces[:top])
    arrived = []
    for k in range(1, subj):
        if k == near_step:
            both, moved = tie(both, moved)
        if k == far_step:
            both, far = tie(both, far)
            far = [far[d * plan.g : (d + 1) * plan.g] for d in range(top)]
            f, ends = forward_lines(plan, place, [*moved, *over_space(plan, far)])
        if k >= ends_step and len(arrived) < half:
            extra = arrived[-1] if arrived else (ends, ends)
            both = tuple(jnp.concatenate([b, e]) for b, e in zip(both, extra))
        both = go_round(both)
        if both[0].shape[0] > plan.late:
            arrived.append(tuple(b[plan.late :] for b in both))
        if k == far_step:
            both, (f, ends) = tie(both, (f, ends))
        if k < subj - 1:
            both = tuple(b[: plan.late] + late[way][k] for way, b in enumerate(both))
    while len(arrived) < half:
        arrived.append(go_round(arrived[-1] if arrived else (ends, ends)))
    all_ends = [ends] + [e for pair in arrived for e in pair]

    f_late, ends_late = late_forward(
        plan, place, late[0][subj - 1 :], late[1][subj - 1 :], *both
    )
    others = [over_one(plan, ends_late, d) for d in range(space)]
    f, others = tie(f, others)
    *back, far = backward_lines(plan, place, f, all_ends[:subj])
    f_late, back[0] = tie(f_late, back[0])
    far = lax.ppermute(far, "space", [(i, i ^ top) for i in range(space)])
    back = over_space(plan, back)
    back_late = late_backward(plan, place, f_late, others)
    back_late, back = tie(back_late, back)
    back_late = lax.all_to_all(back_late, "subj", 0, 0)
    back_late = back_late.reshape(plan.late, plan.lanes)
    far = [far[d * plan.g : (d + 1) * plan.g] for d in range(top)]
    back += over_space(plan, far)
    return finish(plan, place, velocity, [*back, back_late])


def smoothing_symbol(first, second, third, length):
    def damping(freq):
        turns = (freq % length).astype(jnp.float32)
        return 2.0 - 2.0 * jnp.cos(turns * (2.0 * math.pi / length))

    total = damping(first) + damping(second) + damping(third)
    return 1.0 / (1.0 + alpha_reach * total) ** 2


def transposing_body(template_warped, subject_images, jacobians, velocity):
    length = template_warped.shape[3]
    half = length // 2
    warped = template_warped.astype(jnp.float32)
    slope = (jnp.roll(warped, -1, axis=3) - jnp.roll(warped, 1, axis=3)) * 0.5
    partial_value = jnp.sum(
        jacobians.astype(jnp.float32) * (subject_images.astype(jnp.float32) - warped) * slope,
        axis=0,
    )
    forward, inverse, _ = packed_np(length)
    forward, inverse = forward.astype(np.float32), inverse.astype(np.float32)
    packed = jnp.einsum("xyz,zp->xpy", partial_value, forward, precision=highest)
    packed = lax.psum_scatter(packed, "subj", scatter_dimension=1, tiled=True)
    packed = packed * (2.0 / sigma_sq)
    spectra = jnp.einsum("xpy,yk->kpx", packed, forward, precision=highest)
    lines = lax.all_to_all(spectra, "space", split_axis=0, concat_axis=2, tiled=True)
    freq_lines = jnp.einsum("kpx,xw->kpw", lines, forward, precision=highest)

    def true_freq(index):
        return jnp.where(index <= half, index, index - half)

    def mine(axis, size):
        return true_freq(lax.axis_index(axis) * size + jnp.arange(size, dtype=jnp.int32))

    symbol = smoothing_symbol(
        mine("space", lines.shape[0])[:, None, None],
        mine("subj", lines.shape[1])[None, :, None],
        true_freq(jnp.arange(length, dtype=jnp.int32))[None, None, :],
        length,
    )
    back_lines = jnp.einsum("kpw,wx->xpk", freq_lines * symbol, inverse, precision=highest)
    columns = lax.all_to_all(back_lines, "space", split_axis=0, concat_axis=2, tiled=True)
    real_field = jnp.einsum("xpk,ky->xpy", columns, inverse, precision=highest)
    depth_lines = lax.all_to_all(real_field, "subj", split_axis=2, concat_axis=1, tiled=True)
    smoothed = jnp.einsum("xpy,pz->xyz", depth_lines, inverse, precision=highest)
    return velocity - step_size * (2.0 * velocity - smoothed)


def body(subj, space, template_warped, subject_images, jacobians, velocity):
    _, xl, _, length = template_warped.shape
    yl = velocity.shape[1]
    power_of_two = subj & (subj - 1) == 0 and space & (space - 1) == 0
    fits = (
        subj > 1
        and power_of_two
        and length % lane == 0
        and yl % 32 == 0
        and xl >= 16
        and lane % xl == 0
        and 2 * xl == lane
        and early_eighths * length // 8 % (16 * space) == 0
        and space % early_parts == 0
        and early_eighths * length // 8 % (8 * space) == 0
        and (8 - early_eighths) * length // 8 % (8 * subj) == 0
        and yl * xl == 8 * length
    )
    if not fits:
        return transposing_body(template_warped, subject_images, jacobians, velocity)
    plan = Plan(length, xl, subj, space)
    return ring_body(plan, template_warped, subject_images, jacobians, velocity)


def solution(mesh):
    return jax.shard_map(
        functools.partial(body, mesh.shape["subj"], mesh.shape["space"]),
        mesh=mesh,
        in_specs=(
            P("subj", "space", None, None),
            P("subj", "space", None, None),
            P("subj", "space", None, None),
            P("space", "subj", None),
        ),
        out_specs=P("space", "subj", None),
        check_vma=False,
    )
```

```python
import functools
import math

import jax
import jax.numpy as jnp
import ml_dtypes
import numpy as np
from jax import lax
from jax.experimental import pallas as pl
from jax.experimental.pallas import tpu as pltpu
from jax.sharding import PartitionSpec as P

sigma_sq = 0.05
step_size = 0.25
alpha_reach = 16.0
highest = lax.Precision.HIGHEST
vmem_bytes = 50 * 1024 * 1024
lane = 128
early_eighths = 6
early_parts = 2
near_step, far_step, ends_step = 3, 4, 5


def split_bf16(table):
    high = table.astype(ml_dtypes.bfloat16)
    low = (table - high.astype(np.float64)).astype(ml_dtypes.bfloat16)
    return high, low


def packed_np(length):
    half = length // 2
    index = np.arange(length)
    freq = np.where(index <= half, index, index - half)
    angle = (index[:, None] * freq[None, :] % length) * (2.0 * math.pi / length)
    forward = np.where(index[None, :] <= half, np.cos(angle), np.sin(angle))
    weight = np.where((index == 0) | (index == half), 1.0, 2.0) / length
    lam = 2.0 - 2.0 * np.cos(freq * (2.0 * math.pi / length))
    return forward, (forward * weight[None, :]).T, lam


class Plan:
    def __init__(self, length, rows_x, subj, space):
        self.length, self.xl, self.subj, self.space = length, rows_x, subj, space
        self.yl = length // subj
        self.lanes = self.yl * self.xl
        self.half = self.lanes // 2
        self.ty = lane // self.xl if self.xl < lane else 1
        self.tiles = self.lanes // lane
        early = length * early_eighths // 8
        self.early, self.late = early, length - early
        self.chunks = [self.early, self.late]
        self.part = early // early_parts
        self.g, self.gl = self.early // space, self.late // subj
        ring = list(range(0, subj, 2)) + list(range(subj - 1, 0, -2))
        self.ring = ring
        rows = np.zeros((subj, space, 2 * subj + 2), np.int32)
        for at, j in enumerate(ring):
            for k in range(subj):
                rows[j, :, 2 * k] = ring[(at - 1 - k) % subj]
                rows[j, :, 2 * k + 1] = ring[(at + 1 + k) % subj]
            rows[j, :, 2 * subj] = np.arange(space)
            rows[j, :, 2 * subj + 1] = j
        self.place_table = rows
        self.at_space, self.at_subj = 2 * subj, 2 * subj + 1
        forward, inverse, lam = packed_np(length)
        high, low = split_bf16(forward.T)
        self.t_table = np.concatenate([high, high, low], axis=1)
        high, low = split_bf16(inverse)
        self.i_table = np.stack([high, low])
        lines = length // self.ty
        high, low = split_bf16(forward.reshape(lines, self.ty * length))
        self.y_table = np.concatenate([high, high, low], axis=0)
        wide = inverse.T.reshape(lines, self.ty, length).transpose(1, 0, 2)
        high, low = split_bf16(wide.reshape(length, length))
        self.g_table = np.concatenate([high, high, low], axis=1)
        eye = np.eye(self.ty)
        blocks = forward.reshape(space, self.xl, length)
        wide = np.einsum("ab,sxw->saxbw", eye, blocks).reshape(space, lane, self.ty * length)
        high, low = split_bf16(wide)
        self.w_table = np.concatenate([high, high, low], axis=1)
        blocks = inverse.reshape(length, space, self.xl)
        wide = np.einsum("ab,wsx->sawbx", eye, blocks).reshape(space, self.ty * length, lane)
        high, low = split_bf16(wide)
        self.v_table = np.concatenate([high, high, low], axis=1)
        index = np.arange(length)
        slope = np.zeros((length, length))
        slope[(index + 1) % length, index] += 0.5
        slope[(index - 1) % length, index] -= 0.5
        slope = slope.astype(ml_dtypes.bfloat16)
        self.d_table = np.concatenate([slope, self.t_table], axis=1)
        centre = (1.0 + alpha_reach * (lam[:, None] + lam[None, :])) / alpha_reach + 2.0
        r = 2.0 / (centre + np.sqrt(centre * centre - 4.0))
        q = r * r
        scale = (2.0 / sigma_sq) * q / (alpha_reach * alpha_reach)
        table = np.stack([r, scale * (1 + q) / (1 - q) ** 3, scale / (1 - q) ** 2, np.log(r)])
        table = table.astype(np.float32)
        early_rows = table[:, :early].reshape(4, space, self.g, length)
        self.r_early = early_rows.transpose(1, 0, 2, 3)
        late_rows = table[:, early:].reshape(4, subj, self.gl, length)
        self.r_late = late_rows.transpose(1, 0, 2, 3)


def split(value):
    high = value.astype(jnp.bfloat16)
    low = (value - high.astype(jnp.float32)).astype(jnp.bfloat16)
    return high, low


def call_once(kernel, name, out_shape, place, args, scratch=()):
    vmem = pl.BlockSpec(memory_space=pltpu.VMEM)
    return pl.pallas_call(
        kernel,
        out_shape=out_shape,
        in_specs=[pl.BlockSpec(memory_space=pltpu.SMEM)] + [vmem] * len(args),
        out_specs=jax.tree.map(lambda _: vmem, out_shape),
        scratch_shapes=scratch,
        compiler_params=params(),
        name=name,
    )(place, *[jnp.asarray(a) for a in args])


def params(**kw):
    return pltpu.CompilerParams(vmem_limit_bytes=vmem_bytes, **kw)


def force_kernel(plan, place_ref, warped, images, jac, table, *rest):
    outs, field = rest[:-1], rest[-1]
    me = place_ref[plan.at_space]
    n = len(outs) // 2
    way = pl.program_id(0)
    yh = plan.yl // 2
    count = warped.shape[0]
    length = plan.length
    rows = plan.xl * yh

    total = None
    for b in range(count):
        w = warped[b].reshape(rows, length)
        slope = jnp.dot(w, table[:, :length], preferred_element_type=jnp.float32)
        diff = images[b].reshape(rows, length).astype(jnp.float32) - w.astype(jnp.float32)
        term = jac[b].reshape(rows, length).astype(jnp.float32) * diff * slope
        total = term if total is None else total + term
    field[...] = jnp.swapaxes(total.reshape(plan.xl, yh, length), 0, 1)

    def transform(refs):
        starts = [pl.multiple_of((me ^ d) * plan.g, 16) for d in range(plan.space)]
        rows_of = [table[pl.ds(start, plan.g), length:] for start in starts]
        ordered = jnp.concatenate([*rows_of, table[plan.early :, length:]], axis=0)
        per = max(1, 256 // plan.xl)
        for y0 in range(0, yh, per):
            lines = field[y0 : y0 + per].reshape(per * plan.xl, length)
            high, low = split(lines)
            both = jnp.concatenate([high, low, high], axis=1)
            out = lax.dot_general(
                ordered, both, (((1,), (1,)), ((), ())), preferred_element_type=jnp.float32
            )
            cols = slice(y0 * plan.xl, (y0 + per) * plan.xl)
            first = 0
            for ref in refs:
                ref[:, cols] = out[first : first + ref.shape[0]]
                first += ref.shape[0]

    @pl.when(way == 0)
    def _():
        transform(outs[:n])

    @pl.when(way == 1)
    def _():
        transform(outs[n:])


def force_blocks(plan, k, place, warped, images, jac):
    count, xl, _, length = warped.shape
    yh = plan.yl // 2
    source = pl.BlockSpec(
        (count, xl, yh, length), lambda way, place: (0, 0, 2 * place[2 * k + way] + way, 0)
    )
    sizes = [plan.part] * early_parts + [plan.late]
    shapes = [jax.ShapeDtypeStruct((c, plan.half), jnp.float32) for c in sizes] * 2
    outs = pl.pallas_call(
        functools.partial(force_kernel, plan),
        out_shape=shapes,
        grid_spec=pltpu.PrefetchScalarGridSpec(
            num_scalar_prefetch=1,
            grid=(2,),
            in_specs=[
                source,
                source,
                source,
                pl.BlockSpec((length, 4 * length), lambda way, place: (0, 0)),
            ],
            out_specs=[pl.BlockSpec(s.shape, lambda way, place: (0, 0)) for s in shapes],
            scratch_shapes=[pltpu.VMEM((yh, xl, length), jnp.float32)],
        ),
        compiler_params=params(),
        cost_estimate=pl.CostEstimate(
            flops=16 * xl * yh * length * length,
            bytes_accessed=12 * count * xl * yh * length + 8 * xl * yh * length,
            transcendentals=0,
        ),
        name="force",
    )(place, warped, images, jac, jnp.asarray(plan.d_table))
    n = len(sizes)
    return outs[:n], outs[n:]


def join_kernel(plan, place_ref, *rest):
    arrived, outs = rest[: -plan.space], rest[-plan.space :]
    per = plan.part // plan.g
    for d, out in enumerate(outs):
        part, at = d // per, d % per * plan.g
        for way in range(2):
            mine, came = arrived[(2 * part + way) * 2 : (2 * part + way) * 2 + 2]
            cols = slice(way * plan.half, (way + 1) * plan.half)
            out[:, cols] = mine[at : at + plan.g] + came[at : at + plan.g]


def join(plan, place, args):
    return call_once(
        functools.partial(join_kernel, plan),
        "join",
        [jax.ShapeDtypeStruct((plan.g, plan.lanes), jnp.float32)] * plan.space,
        place,
        args,
    )


def regroup_kernel(plan, place_ref, *rest):
    sources, outs = rest[:-2], rest[-2:]
    for n, source in enumerate(sources):
        at = 2 * place_ref[n] + n % 2
        to = pl.ds(pl.multiple_of(at % plan.subj * plan.gl, 8), plan.gl)

        def put(way):
            for m in range(plan.subj):
                target = place_ref[2 * m + way]
                rows = pl.ds(pl.multiple_of(target * plan.gl, 8), plan.gl)
                outs[way][m, to, :] = source[rows, :]

        for way in range(2):
            pl.when(at // plan.subj == way)(functools.partial(put, way))


def regroup(plan, place, sources):
    shape = (plan.subj, plan.late, plan.half)
    return call_once(
        functools.partial(regroup_kernel, plan),
        "regroup",
        [jax.ShapeDtypeStruct(shape, jnp.float32)] * 2,
        place,
        sources,
    )


def forward_kernel(plan, place_ref, r_ref, w_ref, *rest):
    g = plan.g
    pieces, f_ref, ends_ref = rest[: plan.space], rest[-2], rest[-1]
    me = place_ref[plan.at_space]
    total = None
    for d, piece in enumerate(pieces):
        lines = jnp.concatenate(
            [piece[:, t * lane : (t + 1) * lane] for t in range(plan.tiles)], axis=0
        )
        high, low = split(lines)
        both = jnp.concatenate([high, low, high], axis=1)
        term = jnp.dot(both, w_ref[me ^ d], preferred_element_type=jnp.float32)
        total = term if total is None else total + term
    f_ref[...] = total
    r = r_ref[me, 0]
    length = plan.length

    def line(y):
        t, a = y // plan.ty, y % plan.ty
        return f_ref[t * g : (t + 1) * g, a * length : (a + 1) * length]

    zero = jnp.zeros_like(r)
    v, w = zero, zero
    for y in range(plan.yl):
        w = r * (w + v)
        v = line(y) + r * v
    ends_ref[:, :length], ends_ref[:, length : 2 * length] = v, w
    v, w = zero, zero
    for y in range(plan.yl - 1, -1, -1):
        v = v + line(y)
        w = r * (w + v)
        v = r * v
    ends_ref[:, 2 * length : 3 * length], ends_ref[:, 3 * length :] = v, w


def forward_lines(plan, place, pieces):
    return call_once(
        functools.partial(forward_kernel, plan),
        "first_forward",
        [
            jax.ShapeDtypeStruct((plan.tiles * plan.g, plan.ty * plan.length), jnp.float32),
            jax.ShapeDtypeStruct((plan.g, 4 * plan.length), jnp.float32),
        ],
        place,
        [plan.r_early, plan.w_table, *pieces],
    )


def enter(log_r, length, size, blocks, block, sources):
    full = jnp.exp(float(length) * log_r)
    once = 1.0 / (1.0 - full)
    again = float(length) * full * once
    carry = [jnp.zeros_like(log_r)] * 4
    g = log_r.shape[0]
    for source, ref in sources:
        for i in (0, 2):
            between = block - 1 - source if i == 0 else source - 1 - block
            between = jnp.where(between < 0, between + blocks, between)
            reach = (between * size).astype(jnp.float32)
            power = once * jnp.exp(reach * log_r)
            v = ref[:g, i * length : (i + 1) * length]
            w = ref[:g, (i + 1) * length : (i + 2) * length]
            carry[i] = carry[i] + power * v
            carry[i + 1] = carry[i + 1] + power * (w + (reach + again) * v)
    return carry


def backward_kernel(plan, place_ref, r_ref, v_ref, f_ref, *rest):
    ends_refs, outs, u_ref = rest[: plan.subj], rest[plan.subj : -1], rest[-1]
    me, block = place_ref[plan.at_space], place_ref[plan.at_subj]
    g, length = plan.g, plan.length
    r, alpha, beta, log_r = (r_ref[me, i] for i in range(4))
    sources = [(block if h == 0 else place_ref[h - 1], ref) for h, ref in enumerate(ends_refs)]
    carry = enter(log_r, length, plan.yl, plan.subj, block, sources)

    def line(y):
        t, a = y // plan.ty, y % plan.ty
        return (slice(t * g, (t + 1) * g), slice(a * length, (a + 1) * length))

    v, w = carry[0], carry[1]
    for y in range(plan.yl):
        w = r * (w + v)
        v = f_ref[line(y)] + r * v
        u_ref[line(y)] = alpha * v + beta * w
    v, w = carry[2], carry[3]
    for y in range(plan.yl - 1, -1, -1):
        u_ref[line(y)] = u_ref[line(y)] + (alpha * v + beta * w)
        v = v + f_ref[line(y)]
        w = r * (w + v)
        v = r * v
    high, low = split(u_ref[...])
    both = jnp.concatenate([high, low, high], axis=1)
    top = plan.space // 2
    tables = jnp.concatenate([v_ref[me ^ d] for d in range(plan.space)], axis=1)
    all_back = jnp.dot(both, tables, preferred_element_type=jnp.float32)
    for d in range(plan.space):
        out = outs[min(d, top)]
        first = max(d - top, 0) * g
        back = all_back[:, d * lane : (d + 1) * lane]
        for t in range(plan.tiles):
            out[first : first + g, t * lane : (t + 1) * lane] = back[t * g : (t + 1) * g]


def backward_lines(plan, place, f, ends):
    top = plan.space // 2
    counts = [plan.g] * top + [plan.g * top]
    return call_once(
        functools.partial(backward_kernel, plan),
        "second_and_back",
        [jax.ShapeDtypeStruct((c, plan.lanes), jnp.float32) for c in counts],
        place,
        [plan.r_early, plan.v_table, f, *ends],
        scratch=[pltpu.VMEM(f.shape, jnp.float32)],
    )


def late_forward_kernel(plan, place_ref, r_ref, y_ref, *rest):
    *arrived, f_ref, ends_ref, z_ref = rest
    length, gl, xl, ty = plan.length, plan.gl, plan.xl, plan.ty
    lines = length // ty
    tiles = plan.half // lane
    for way in range(2):
        local, ref = arrived[way], arrived[2 + way]
        for b in range(plan.subj):
            rows = slice(b * gl, (b + 1) * gl)
            for t in range(tiles):
                cols = slice(t * lane, (t + 1) * lane)
                to = ((way * plan.subj + b) * tiles + t) * gl
                z_ref[to : to + gl, :] = ref[rows, cols] + local[0, rows, cols]
    turned = jnp.concatenate([z_ref[pl.ds(p, lines, stride=gl), :].T for p in range(gl)], axis=0)
    high, low = split(turned)
    both = jnp.concatenate([high, low, high], axis=1)
    out = jnp.dot(both, y_ref[...], preferred_element_type=jnp.float32)
    for p in range(gl):
        value = None
        for a in range(ty):
            rows = slice(p * lane + a * xl, p * lane + (a + 1) * xl)
            term = out[rows, a * length : (a + 1) * length]
            value = term if value is None else value + term
        for h in range(length // lane):
            f_ref[h, pl.ds(p, xl, stride=gl), :] = value[:, h * lane : (h + 1) * lane]
    r = r_ref[place_ref[plan.at_subj], 0]

    def line(x):
        rows = slice(x * gl, (x + 1) * gl)
        return jnp.concatenate([f_ref[h, rows, :] for h in range(length // lane)], axis=1)

    zero = jnp.zeros_like(r)
    v, w = zero, zero
    for x in range(xl):
        w = r * (w + v)
        v = line(x) + r * v
    ends_ref[:, :length], ends_ref[:, length : 2 * length] = v, w
    v, w = zero, zero
    for x in range(xl - 1, -1, -1):
        v = v + line(x)
        w = r * (w + v)
        v = r * v
    ends_ref[:, 2 * length : 3 * length], ends_ref[:, 3 * length :] = v, w


def late_forward(plan, place, *args):
    return call_once(
        functools.partial(late_forward_kernel, plan),
        "second_forward",
        [
            jax.ShapeDtypeStruct((plan.length // lane, plan.xl * plan.gl, lane), jnp.float32),
            jax.ShapeDtypeStruct((plan.gl, 4 * plan.length), jnp.float32),
        ],
        place,
        [plan.r_late, plan.y_table, *args],
        scratch=[pltpu.VMEM((plan.length // plan.ty * plan.gl, lane), jnp.float32)],
    )


def late_backward_kernel(plan, place_ref, r_ref, g_ref, f_ref, *rest):
    ends_refs = rest[: plan.space]
    out_ref, u_ref, y_ref = rest[plan.space :]
    me = place_ref[plan.at_space]
    length, gl, xl, ty = plan.length, plan.gl, plan.xl, plan.ty
    lines, halves = length // ty, length // lane
    r, alpha, beta, log_r = (r_ref[place_ref[plan.at_subj], i] for i in range(4))
    sources = [(me ^ d, ref) for d, ref in enumerate(ends_refs)]
    carry = enter(log_r, length, xl, plan.space, me, sources)

    def line(ref, x):
        rows = slice(x * gl, (x + 1) * gl)
        return jnp.concatenate([ref[h, rows, :] for h in range(halves)], axis=1)

    def keep(x, value):
        for h in range(halves):
            u_ref[h, x * gl : (x + 1) * gl, :] = value[:, h * lane : (h + 1) * lane]

    v, w = carry[0], carry[1]
    for x in range(xl):
        w = r * (w + v)
        v = line(f_ref, x) + r * v
        keep(x, alpha * v + beta * w)
    v, w = carry[2], carry[3]
    for x in range(xl - 1, -1, -1):
        keep(x, line(u_ref, x) + (alpha * v + beta * w))
        v = v + line(f_ref, x)
        w = r * (w + v)
        v = r * v
    rows = jnp.concatenate(
        [
            jnp.concatenate(
                [u_ref[h, pl.ds(p, xl, stride=gl), :] for h in range(halves)], axis=1
            )
            for p in range(gl)
        ],
        axis=0,
    )
    high, low = split(rows)
    both = jnp.concatenate([high, low, high], axis=1)
    out = lax.dot_general(
        g_ref[...], both, (((1,), (1,)), ((), ())), preferred_element_type=jnp.float32
    )
    place_of = lax.broadcasted_iota(jnp.int32, (lines, lane), 1) // xl
    for p in range(gl):
        tile, spot = p // ty, p % ty
        value = None
        for a in range(ty):
            part = out[a * lines : (a + 1) * lines, tile * lane : (tile + 1) * lane]
            if a != spot:
                part = pltpu.roll(part, (a - spot) % ty * xl, 1)
            value = part if value is None else jnp.where(place_of == a, part, value)
        y_ref[pl.ds(p, lines, stride=gl), :] = value
    for j in range(plan.subj):
        for t in range(plan.tiles):
            start = (j * plan.tiles + t) * gl
            out_ref[j, :, t * lane : (t + 1) * lane] = y_ref[start : start + gl, :]


def late_backward(plan, place, f, ends):
    return call_once(
        functools.partial(late_backward_kernel, plan),
        "first_and_back",
        jax.ShapeDtypeStruct((plan.subj, plan.gl, plan.lanes), jnp.float32),
        place,
        [plan.r_late, plan.g_table, f, *ends],
        scratch=[
            pltpu.VMEM(f.shape, jnp.float32),
            pltpu.VMEM((plan.length // plan.ty * plan.gl, lane), jnp.float32),
        ],
    )


def finish_kernel(plan, y_step, place_ref, i_ref, velocity, *rest):
    pieces, out = rest[:-1], rest[-1]
    length, xl = plan.length, plan.xl
    me = place_ref[plan.at_space]
    starts = [pl.multiple_of((me ^ d) * plan.g, 8) for d in range(plan.space)]
    high, low = (
        jnp.concatenate(
            [i_ref[i, pl.ds(start, plan.g), :] for start in starts] + [i_ref[i, plan.early :, :]],
            axis=0,
        )
        for i in range(2)
    )
    table = jnp.concatenate([high, high, low], axis=0)
    lines = []
    for t in range(y_step // plan.ty):
        columns = jnp.concatenate([p[:, t * lane : (t + 1) * lane] for p in pieces], axis=0)
        high, low = split(columns.T)
        both = jnp.concatenate([high, low, high], axis=1)
        lines.append(jnp.dot(both, table, preferred_element_type=jnp.float32))
        if len(lines) * plan.ty == 8:
            y = (t + 1) * plan.ty - 8
            block = jnp.concatenate(lines, axis=0).reshape(8, xl, length)
            smoothed = jnp.swapaxes(block, 0, 1)
            vel = velocity[:, y : y + 8, :]
            out[:, y : y + 8, :] = vel - step_size * (2.0 * vel - smoothed)
            lines = []


def finish(plan, place, velocity, pieces):
    xl, yl, length = velocity.shape
    y_step = 16
    width = y_step * xl
    block = pl.BlockSpec((xl, y_step, length), lambda at, place: (0, at, 0))
    return pl.pallas_call(
        functools.partial(finish_kernel, plan, y_step),
        out_shape=jax.ShapeDtypeStruct(velocity.shape, jnp.float32),
        grid_spec=pltpu.PrefetchScalarGridSpec(
            num_scalar_prefetch=1,
            grid=(yl // y_step,),
            in_specs=[
                pl.BlockSpec((2, length, length), lambda at, place: (0, 0, 0)),
                block,
            ]
            + [pl.BlockSpec((p.shape[0], width), lambda at, place: (0, at)) for p in pieces],
            out_specs=block,
        ),
        compiler_params=params(),
        name="last_back",
    )(place, jnp.asarray(plan.i_table), velocity, *pieces)


def tie(first, second):
    return lax.optimization_barrier((first, second))


def over_one(plan, part, d):
    if d == 0:
        return part
    return lax.ppermute(part, "space", [(i, i ^ d) for i in range(plan.space)])


def over_space(plan, pieces):
    return [over_one(plan, piece, d) for d, piece in enumerate(pieces)]


def ring_body(plan, template_warped, subject_images, jacobians, velocity):
    subj, space, half = plan.subj, plan.space, plan.subj // 2
    j, s = lax.axis_index("subj"), lax.axis_index("space")
    table = plan.place_table
    place = lax.dynamic_slice(jnp.asarray(table), (j, s, 0), (1, 1, table.shape[2])).reshape(-1)
    to_right = [(plan.ring[i], plan.ring[(i + 1) % subj]) for i in range(subj)]
    to_left = [(b, a) for a, b in to_right]

    def go_round(both):
        return lax.ppermute(both[0], "subj", to_right), lax.ppermute(both[1], "subj", to_left)

    local = [
        force_blocks(plan, k, place, template_warped, subject_images, jacobians)
        for k in range(subj)
    ]

    parts = range(early_parts)
    streams = [(local[0][0][p], local[0][1][p]) for p in parts]
    for k in range(1, subj):
        streams = [go_round(both) for both in streams]
        if k < subj - 1:
            streams = [
                tuple(b + local[k][way][p] for way, b in enumerate(both))
                for p, both in enumerate(streams)
            ]
    late = regroup(plan, place, [local[k][way][-1] for k in range(subj) for way in range(2)])
    both, streams = tie((late[0][0], late[1][0]), streams)
    pieces = join(
        plan, place, [a for p in parts for way in range(2) for a in (local[-1][way][p], streams[p][way])]
    )

    top = space // 2
    far = lax.ppermute(
        jnp.concatenate(pieces[top:]), "space", [(i, i ^ top) for i in range(space)]
    )
    moved = over_space(plan, pieces[:top])
    arrived = []
    for k in range(1, subj):
        if k == near_step:
            both, moved = tie(both, moved)
        if k == far_step:
            far = over_space(plan, [far[d * plan.g : (d + 1) * plan.g] for d in range(top)])
            both, far = tie(both, far)
            f, ends = forward_lines(plan, place, [*moved, *far])
        if k >= ends_step and len(arrived) < half:
            extra = arrived[-1] if arrived else (ends, ends)
            both = tuple(jnp.concatenate([b, e]) for b, e in zip(both, extra))
        both = go_round(both)
        if both[0].shape[0] > plan.late:
            arrived.append(tuple(b[plan.late :] for b in both))
        if k == far_step:
            both, (f, ends) = tie(both, (f, ends))
        if k < subj - 1:
            both = tuple(b[: plan.late] + late[way][k] for way, b in enumerate(both))
    while len(arrived) < half:
        arrived.append(go_round(arrived[-1] if arrived else (ends, ends)))
    all_ends = [ends] + [e for pair in arrived for e in pair]

    f_late, ends_late = late_forward(
        plan, place, late[0][subj - 1 :], late[1][subj - 1 :], *both
    )
    others = [over_one(plan, ends_late, d) for d in range(space)]
    f, others = tie(f, others)
    *back, far = backward_lines(plan, place, f, all_ends[:subj])
    f_late, back[0] = tie(f_late, back[0])
    far = lax.ppermute(far, "space", [(i, i ^ top) for i in range(space)])
    back = over_space(plan, back)
    back_late = late_backward(plan, place, f_late, others)
    back_late, back = tie(back_late, back)
    back_late = lax.all_to_all(back_late, "subj", 0, 0)
    back_late = back_late.reshape(plan.late, plan.lanes)
    far = [far[d * plan.g : (d + 1) * plan.g] for d in range(top)]
    back += over_space(plan, far)
    return finish(plan, place, velocity, [*back, back_late])


def smoothing_symbol(first, second, third, length):
    def damping(freq):
        turns = (freq % length).astype(jnp.float32)
        return 2.0 - 2.0 * jnp.cos(turns * (2.0 * math.pi / length))

    total = damping(first) + damping(second) + damping(third)
    return 1.0 / (1.0 + alpha_reach * total) ** 2


def transposing_body(template_warped, subject_images, jacobians, velocity):
    length = template_warped.shape[3]
    half = length // 2
    warped = template_warped.astype(jnp.float32)
    slope = (jnp.roll(warped, -1, axis=3) - jnp.roll(warped, 1, axis=3)) * 0.5
    partial_value = jnp.sum(
        jacobians.astype(jnp.float32) * (subject_images.astype(jnp.float32) - warped) * slope,
        axis=0,
    )
    forward, inverse, _ = packed_np(length)
    forward, inverse = forward.astype(np.float32), inverse.astype(np.float32)
    packed = jnp.einsum("xyz,zp->xpy", partial_value, forward, precision=highest)
    packed = lax.psum_scatter(packed, "subj", scatter_dimension=1, tiled=True)
    packed = packed * (2.0 / sigma_sq)
    spectra = jnp.einsum("xpy,yk->kpx", packed, forward, precision=highest)
    lines = lax.all_to_all(spectra, "space", split_axis=0, concat_axis=2, tiled=True)
    freq_lines = jnp.einsum("kpx,xw->kpw", lines, forward, precision=highest)

    def true_freq(index):
        return jnp.where(index <= half, index, index - half)

    def mine(axis, size):
        return true_freq(lax.axis_index(axis) * size + jnp.arange(size, dtype=jnp.int32))

    symbol = smoothing_symbol(
        mine("space", lines.shape[0])[:, None, None],
        mine("subj", lines.shape[1])[None, :, None],
        true_freq(jnp.arange(length, dtype=jnp.int32))[None, None, :],
        length,
    )
    back_lines = jnp.einsum("kpw,wx->xpk", freq_lines * symbol, inverse, precision=highest)
    columns = lax.all_to_all(back_lines, "space", split_axis=0, concat_axis=2, tiled=True)
    real_field = jnp.einsum("xpk,ky->xpy", columns, inverse, precision=highest)
    depth_lines = lax.all_to_all(real_field, "subj", split_axis=2, concat_axis=1, tiled=True)
    smoothed = jnp.einsum("xpy,pz->xyz", depth_lines, inverse, precision=highest)
    return velocity - step_size * (2.0 * velocity - smoothed)


def body(subj, space, template_warped, subject_images, jacobians, velocity):
    _, xl, _, length = template_warped.shape
    yl = velocity.shape[1]
    power_of_two = subj & (subj - 1) == 0 and space & (space - 1) == 0
    fits = (
        subj > 1
        and power_of_two
        and length % lane == 0
        and yl % 32 == 0
        and xl >= 16
        and lane % xl == 0
        and 2 * xl == lane
        and early_eighths * length // 8 % (16 * space) == 0
        and space % early_parts == 0
        and early_eighths * length // 8 % (8 * space) == 0
        and (8 - early_eighths) * length // 8 % (8 * subj) == 0
        and yl * xl == 8 * length
    )
    if not fits:
        return transposing_body(template_warped, subject_images, jacobians, velocity)
    plan = Plan(length, xl, subj, space)
    return ring_body(plan, template_warped, subject_images, jacobians, velocity)


def solution(mesh):
    return jax.shard_map(
        functools.partial(body, mesh.shape["subj"], mesh.shape["space"]),
        mesh=mesh,
        in_specs=(
            P("subj", "space", None, None),
            P("subj", "space", None, None),
            P("subj", "space", None, None),
            P("space", "subj", None),
        ),
        out_specs=P("space", "subj", None),
        check_vma=False,
    )
```

```python
import functools
import math

import jax
import jax.numpy as jnp
import ml_dtypes
import numpy as np
from jax import lax
from jax.experimental import pallas as pl
from jax.experimental.pallas import tpu as pltpu
from jax.sharding import PartitionSpec as P

sigma_sq = 0.05
step_size = 0.25
alpha_reach = 16.0
highest = lax.Precision.HIGHEST
vmem_bytes = 50 * 1024 * 1024
lane = 128
early_eighths = 6
early_parts = 2
near_step, far_step, ends_step = 3, 4, 5


def split_bf16(table):
    high = table.astype(ml_dtypes.bfloat16)
    low = (table - high.astype(np.float64)).astype(ml_dtypes.bfloat16)
    return high, low


def packed_np(length):
    half = length // 2
    index = np.arange(length)
    freq = np.where(index <= half, index, index - half)
    angle = (index[:, None] * freq[None, :] % length) * (2.0 * math.pi / length)
    forward = np.where(index[None, :] <= half, np.cos(angle), np.sin(angle))
    weight = np.where((index == 0) | (index == half), 1.0, 2.0) / length
    lam = 2.0 - 2.0 * np.cos(freq * (2.0 * math.pi / length))
    return forward, (forward * weight[None, :]).T, lam


class Plan:
    def __init__(self, length, rows_x, subj, space):
        self.length, self.xl, self.subj, self.space = length, rows_x, subj, space
        self.yl = length // subj
        self.lanes = self.yl * self.xl
        self.half = self.lanes // 2
        self.ty = lane // self.xl if self.xl < lane else 1
        self.tiles = self.lanes // lane
        early = length * early_eighths // 8
        self.early, self.late = early, length - early
        self.chunks = [self.early, self.late]
        self.part = early // early_parts
        self.g, self.gl = self.early // space, self.late // subj
        ring = list(range(0, subj, 2)) + list(range(subj - 1, 0, -2))
        self.ring = ring
        rows = np.zeros((subj, space, 2 * subj + 2), np.int32)
        for at, j in enumerate(ring):
            for k in range(subj):
                rows[j, :, 2 * k] = ring[(at - 1 - k) % subj]
                rows[j, :, 2 * k + 1] = ring[(at + 1 + k) % subj]
            rows[j, :, 2 * subj] = np.arange(space)
            rows[j, :, 2 * subj + 1] = j
        self.place_table = rows
        self.at_space, self.at_subj = 2 * subj, 2 * subj + 1
        forward, inverse, lam = packed_np(length)
        high, low = split_bf16(forward.T)
        self.t_table = np.concatenate([high, high, low], axis=1)
        high, low = split_bf16(inverse)
        self.i_table = np.stack([high, low])
        lines = length // self.ty
        high, low = split_bf16(forward.reshape(lines, self.ty * length))
        self.y_table = np.concatenate([high, high, low], axis=0)
        wide = inverse.T.reshape(lines, self.ty, length).transpose(1, 0, 2)
        high, low = split_bf16(wide.reshape(length, length))
        self.g_table = np.concatenate([high, high, low], axis=1)
        eye = np.eye(self.ty)
        blocks = forward.reshape(space, self.xl, length)
        wide = np.einsum("ab,sxw->saxbw", eye, blocks).reshape(space, lane, self.ty * length)
        high, low = split_bf16(wide)
        self.w_table = np.concatenate([high, high, low], axis=1)
        blocks = inverse.reshape(length, space, self.xl)
        wide = np.einsum("ab,wsx->sawbx", eye, blocks).reshape(space, self.ty * length, lane)
        high, low = split_bf16(wide)
        self.v_table = np.concatenate([high, high, low], axis=1)
        index = np.arange(length)
        slope = np.zeros((length, length))
        slope[(index + 1) % length, index] += 0.5
        slope[(index - 1) % length, index] -= 0.5
        slope = slope.astype(ml_dtypes.bfloat16)
        self.d_table = np.concatenate([slope, self.t_table], axis=1)
        centre = (1.0 + alpha_reach * (lam[:, None] + lam[None, :])) / alpha_reach + 2.0
        r = 2.0 / (centre + np.sqrt(centre * centre - 4.0))
        q = r * r
        scale = (2.0 / sigma_sq) * q / (alpha_reach * alpha_reach)
        table = np.stack([r, scale * (1 + q) / (1 - q) ** 3, scale / (1 - q) ** 2, np.log(r)])
        table = table.astype(np.float32)
        early_rows = table[:, :early].reshape(4, space, self.g, length)
        self.r_early = early_rows.transpose(1, 0, 2, 3)
        late_rows = table[:, early:].reshape(4, subj, self.gl, length)
        self.r_late = late_rows.transpose(1, 0, 2, 3)


def split(value):
    high = value.astype(jnp.bfloat16)
    low = (value - high.astype(jnp.float32)).astype(jnp.bfloat16)
    return high, low


def call_once(kernel, name, out_shape, place, args, scratch=(), cost=None):
    vmem = pl.BlockSpec(memory_space=pltpu.VMEM)
    return pl.pallas_call(
        kernel,
        out_shape=out_shape,
        in_specs=[pl.BlockSpec(memory_space=pltpu.SMEM)] + [vmem] * len(args),
        out_specs=jax.tree.map(lambda _: vmem, out_shape),
        scratch_shapes=scratch,
        compiler_params=params(),
        cost_estimate=cost,
        name=name,
    )(place, *[jnp.asarray(a) for a in args])


def params(**kw):
    return pltpu.CompilerParams(vmem_limit_bytes=vmem_bytes, **kw)


def force_kernel(plan, place_ref, warped, images, jac, table, *rest):
    outs, field = rest[:-1], rest[-1]
    me = place_ref[plan.at_space]
    n = len(outs) // 2
    way = pl.program_id(0)
    yh = plan.yl // 2
    count = warped.shape[0]
    length = plan.length
    rows = plan.xl * yh

    total = None
    for b in range(count):
        w = warped[b].reshape(rows, length)
        slope = jnp.dot(w, table[:, :length], preferred_element_type=jnp.float32)
        diff = images[b].reshape(rows, length).astype(jnp.float32) - w.astype(jnp.float32)
        term = jac[b].reshape(rows, length).astype(jnp.float32) * diff * slope
        total = term if total is None else total + term
    field[...] = jnp.swapaxes(total.reshape(plan.xl, yh, length), 0, 1)

    def transform(refs):
        starts = [pl.multiple_of((me ^ d) * plan.g, 16) for d in range(plan.space)]
        rows_of = [table[pl.ds(start, plan.g), length:] for start in starts]
        ordered = jnp.concatenate([*rows_of, table[plan.early :, length:]], axis=0)
        per = max(1, 256 // plan.xl)
        for y0 in range(0, yh, per):
            lines = field[y0 : y0 + per].reshape(per * plan.xl, length)
            high, low = split(lines)
            both = jnp.concatenate([high, low, high], axis=1)
            out = lax.dot_general(
                ordered, both, (((1,), (1,)), ((), ())), preferred_element_type=jnp.float32
            )
            cols = slice(y0 * plan.xl, (y0 + per) * plan.xl)
            first = 0
            for ref in refs:
                ref[:, cols] = out[first : first + ref.shape[0]]
                first += ref.shape[0]

    @pl.when(way == 0)
    def _():
        transform(outs[:n])

    @pl.when(way == 1)
    def _():
        transform(outs[n:])


def force_blocks(plan, k, place, warped, images, jac):
    count, xl, _, length = warped.shape
    yh = plan.yl // 2
    source = pl.BlockSpec(
        (count, xl, yh, length), lambda way, place: (0, 0, 2 * place[2 * k + way] + way, 0)
    )
    sizes = [plan.part] * early_parts + [plan.late]
    shapes = [jax.ShapeDtypeStruct((c, plan.half), jnp.float32) for c in sizes] * 2
    outs = pl.pallas_call(
        functools.partial(force_kernel, plan),
        out_shape=shapes,
        grid_spec=pltpu.PrefetchScalarGridSpec(
            num_scalar_prefetch=1,
            grid=(2,),
            in_specs=[
                source,
                source,
                source,
                pl.BlockSpec((length, 4 * length), lambda way, place: (0, 0)),
            ],
            out_specs=[pl.BlockSpec(s.shape, lambda way, place: (0, 0)) for s in shapes],
            scratch_shapes=[pltpu.VMEM((yh, xl, length), jnp.float32)],
        ),
        compiler_params=params(),
        cost_estimate=pl.CostEstimate(
            flops=16 * xl * yh * length * length,
            bytes_accessed=12 * count * xl * yh * length + 8 * xl * yh * length,
            transcendentals=0,
        ),
        name="force",
    )(place, warped, images, jac, jnp.asarray(plan.d_table))
    n = len(sizes)
    return outs[:n], outs[n:]


def join_kernel(plan, place_ref, *rest):
    arrived, outs = rest[: -plan.space], rest[-plan.space :]
    per = plan.part // plan.g
    for d, out in enumerate(outs):
        part, at = d // per, d % per * plan.g
        for way in range(2):
            mine, came = arrived[(2 * part + way) * 2 : (2 * part + way) * 2 + 2]
            cols = slice(way * plan.half, (way + 1) * plan.half)
            out[:, cols] = mine[at : at + plan.g] + came[at : at + plan.g]


def join(plan, place, args):
    return call_once(
        functools.partial(join_kernel, plan),
        "join",
        [jax.ShapeDtypeStruct((plan.g, plan.lanes), jnp.float32)] * plan.space,
        place,
        args,
    )


def regroup_kernel(plan, place_ref, *rest):
    sources, outs = rest[:-2], rest[-2:]
    for n, source in enumerate(sources):
        at = 2 * place_ref[n] + n % 2
        to = pl.ds(pl.multiple_of(at % plan.subj * plan.gl, 8), plan.gl)

        def put(way):
            for m in range(plan.subj):
                target = place_ref[2 * m + way]
                rows = pl.ds(pl.multiple_of(target * plan.gl, 8), plan.gl)
                outs[way][m, to, :] = source[rows, :]

        for way in range(2):
            pl.when(at // plan.subj == way)(functools.partial(put, way))


def regroup(plan, place, sources):
    shape = (plan.subj, plan.late, plan.half)
    return call_once(
        functools.partial(regroup_kernel, plan),
        "regroup",
        [jax.ShapeDtypeStruct(shape, jnp.float32)] * 2,
        place,
        sources,
    )


def forward_kernel(plan, place_ref, r_ref, w_ref, *rest):
    g = plan.g
    pieces, f_ref, ends_ref = rest[: plan.space], rest[-2], rest[-1]
    me = place_ref[plan.at_space]
    total = None
    for d, piece in enumerate(pieces):
        lines = jnp.concatenate(
            [piece[:, t * lane : (t + 1) * lane] for t in range(plan.tiles)], axis=0
        )
        high, low = split(lines)
        both = jnp.concatenate([high, low, high], axis=1)
        term = jnp.dot(both, w_ref[me ^ d], preferred_element_type=jnp.float32)
        total = term if total is None else total + term
    f_ref[...] = total
    r = r_ref[me, 0]
    length = plan.length

    def line(y):
        t, a = y // plan.ty, y % plan.ty
        return f_ref[t * g : (t + 1) * g, a * length : (a + 1) * length]

    zero = jnp.zeros_like(r)
    v, w = zero, zero
    for y in range(plan.yl):
        w = r * (w + v)
        v = line(y) + r * v
    ends_ref[:, :length], ends_ref[:, length : 2 * length] = v, w
    v, w = zero, zero
    for y in range(plan.yl - 1, -1, -1):
        v = v + line(y)
        w = r * (w + v)
        v = r * v
    ends_ref[:, 2 * length : 3 * length], ends_ref[:, 3 * length :] = v, w


def forward_lines(plan, place, pieces):
    return call_once(
        functools.partial(forward_kernel, plan),
        "first_forward",
        [
            jax.ShapeDtypeStruct((plan.tiles * plan.g, plan.ty * plan.length), jnp.float32),
            jax.ShapeDtypeStruct((plan.g, 4 * plan.length), jnp.float32),
        ],
        place,
        [plan.r_early, plan.w_table, *pieces],
        cost=pl.CostEstimate(
            flops=6 * plan.tiles * plan.g * plan.ty * plan.length * plan.space * lane,
            bytes_accessed=8 * sum(p.size for p in pieces),
            transcendentals=0,
        ),
    )


def enter(log_r, length, size, blocks, block, sources):
    full = jnp.exp(float(length) * log_r)
    once = 1.0 / (1.0 - full)
    again = float(length) * full * once
    carry = [jnp.zeros_like(log_r)] * 4
    g = log_r.shape[0]
    for source, ref in sources:
        for i in (0, 2):
            between = block - 1 - source if i == 0 else source - 1 - block
            between = jnp.where(between < 0, between + blocks, between)
            reach = (between * size).astype(jnp.float32)
            power = once * jnp.exp(reach * log_r)
            v = ref[:g, i * length : (i + 1) * length]
            w = ref[:g, (i + 1) * length : (i + 2) * length]
            carry[i] = carry[i] + power * v
            carry[i + 1] = carry[i + 1] + power * (w + (reach + again) * v)
    return carry


def backward_kernel(plan, place_ref, r_ref, v_ref, f_ref, *rest):
    ends_refs, outs, u_ref = rest[: plan.subj], rest[plan.subj : -1], rest[-1]
    me, block = place_ref[plan.at_space], place_ref[plan.at_subj]
    g, length = plan.g, plan.length
    r, alpha, beta, log_r = (r_ref[me, i] for i in range(4))
    sources = [(block if h == 0 else place_ref[h - 1], ref) for h, ref in enumerate(ends_refs)]
    carry = enter(log_r, length, plan.yl, plan.subj, block, sources)

    def line(y):
        t, a = y // plan.ty, y % plan.ty
        return (slice(t * g, (t + 1) * g), slice(a * length, (a + 1) * length))

    v, w = carry[0], carry[1]
    for y in range(plan.yl):
        w = r * (w + v)
        v = f_ref[line(y)] + r * v
        u_ref[line(y)] = alpha * v + beta * w
    v, w = carry[2], carry[3]
    for y in range(plan.yl - 1, -1, -1):
        u_ref[line(y)] = u_ref[line(y)] + (alpha * v + beta * w)
        v = v + f_ref[line(y)]
        w = r * (w + v)
        v = r * v
    high, low = split(u_ref[...])
    both = jnp.concatenate([high, low, high], axis=1)
    top = plan.space // 2
    tables = jnp.concatenate([v_ref[me ^ d] for d in range(plan.space)], axis=1)
    all_back = jnp.dot(both, tables, preferred_element_type=jnp.float32)
    for d in range(plan.space):
        out = outs[min(d, top)]
        first = max(d - top, 0) * g
        back = all_back[:, d * lane : (d + 1) * lane]
        for t in range(plan.tiles):
            out[first : first + g, t * lane : (t + 1) * lane] = back[t * g : (t + 1) * g]


def backward_lines(plan, place, f, ends):
    top = plan.space // 2
    counts = [plan.g] * top + [plan.g * top]
    return call_once(
        functools.partial(backward_kernel, plan),
        "second_and_back",
        [jax.ShapeDtypeStruct((c, plan.lanes), jnp.float32) for c in counts],
        place,
        [plan.r_early, plan.v_table, f, *ends],
        scratch=[pltpu.VMEM(f.shape, jnp.float32)],
        cost=pl.CostEstimate(
            flops=6 * f.shape[0] * f.shape[1] * plan.space * lane,
            bytes_accessed=4 * (2 * f.size + sum(e.size for e in ends)),
            transcendentals=0,
        ),
    )


def late_forward_kernel(plan, place_ref, r_ref, y_ref, *rest):
    *arrived, f_ref, ends_ref, z_ref = rest
    length, gl, xl, ty = plan.length, plan.gl, plan.xl, plan.ty
    lines = length // ty
    tiles = plan.half // lane
    for way in range(2):
        local, ref = arrived[way], arrived[2 + way]
        for b in range(plan.subj):
            rows = slice(b * gl, (b + 1) * gl)
            for t in range(tiles):
                cols = slice(t * lane, (t + 1) * lane)
                to = ((way * plan.subj + b) * tiles + t) * gl
                z_ref[to : to + gl, :] = ref[rows, cols] + local[0, rows, cols]
    turned = jnp.concatenate([z_ref[pl.ds(p, lines, stride=gl), :].T for p in range(gl)], axis=0)
    high, low = split(turned)
    both = jnp.concatenate([high, low, high], axis=1)
    out = jnp.dot(both, y_ref[...], preferred_element_type=jnp.float32)
    for p in range(gl):
        value = None
        for a in range(ty):
            rows = slice(p * lane + a * xl, p * lane + (a + 1) * xl)
            term = out[rows, a * length : (a + 1) * length]
            value = term if value is None else value + term
        for h in range(length // lane):
            f_ref[h, pl.ds(p, xl, stride=gl), :] = value[:, h * lane : (h + 1) * lane]
    r = r_ref[place_ref[plan.at_subj], 0]

    def line(x):
        rows = slice(x * gl, (x + 1) * gl)
        return jnp.concatenate([f_ref[h, rows, :] for h in range(length // lane)], axis=1)

    zero = jnp.zeros_like(r)
    v, w = zero, zero
    for x in range(xl):
        w = r * (w + v)
        v = line(x) + r * v
    ends_ref[:, :length], ends_ref[:, length : 2 * length] = v, w
    v, w = zero, zero
    for x in range(xl - 1, -1, -1):
        v = v + line(x)
        w = r * (w + v)
        v = r * v
    ends_ref[:, 2 * length : 3 * length], ends_ref[:, 3 * length :] = v, w


def late_forward(plan, place, *args):
    return call_once(
        functools.partial(late_forward_kernel, plan),
        "second_forward",
        [
            jax.ShapeDtypeStruct((plan.length // lane, plan.xl * plan.gl, lane), jnp.float32),
            jax.ShapeDtypeStruct((plan.gl, 4 * plan.length), jnp.float32),
        ],
        place,
        [plan.r_late, plan.y_table, *args],
        scratch=[pltpu.VMEM((plan.length // plan.ty * plan.gl, lane), jnp.float32)],
    )


def late_backward_kernel(plan, place_ref, r_ref, g_ref, f_ref, *rest):
    ends_refs = rest[: plan.space]
    out_ref, u_ref, y_ref = rest[plan.space :]
    me = place_ref[plan.at_space]
    length, gl, xl, ty = plan.length, plan.gl, plan.xl, plan.ty
    lines, halves = length // ty, length // lane
    r, alpha, beta, log_r = (r_ref[place_ref[plan.at_subj], i] for i in range(4))
    sources = [(me ^ d, ref) for d, ref in enumerate(ends_refs)]
    carry = enter(log_r, length, xl, plan.space, me, sources)

    def line(ref, x):
        rows = slice(x * gl, (x + 1) * gl)
        return jnp.concatenate([ref[h, rows, :] for h in range(halves)], axis=1)

    def keep(x, value):
        for h in range(halves):
            u_ref[h, x * gl : (x + 1) * gl, :] = value[:, h * lane : (h + 1) * lane]

    v, w = carry[0], carry[1]
    for x in range(xl):
        w = r * (w + v)
        v = line(f_ref, x) + r * v
        keep(x, alpha * v + beta * w)
    v, w = carry[2], carry[3]
    for x in range(xl - 1, -1, -1):
        keep(x, line(u_ref, x) + (alpha * v + beta * w))
        v = v + line(f_ref, x)
        w = r * (w + v)
        v = r * v
    rows = jnp.concatenate(
        [
            jnp.concatenate(
                [u_ref[h, pl.ds(p, xl, stride=gl), :] for h in range(halves)], axis=1
            )
            for p in range(gl)
        ],
        axis=0,
    )
    high, low = split(rows)
    both = jnp.concatenate([high, low, high], axis=1)
    out = lax.dot_general(
        g_ref[...], both, (((1,), (1,)), ((), ())), preferred_element_type=jnp.float32
    )
    place_of = lax.broadcasted_iota(jnp.int32, (lines, lane), 1) // xl
    for p in range(gl):
        tile, spot = p // ty, p % ty
        value = None
        for a in range(ty):
            part = out[a * lines : (a + 1) * lines, tile * lane : (tile + 1) * lane]
            if a != spot:
                part = pltpu.roll(part, (a - spot) % ty * xl, 1)
            value = part if value is None else jnp.where(place_of == a, part, value)
        y_ref[pl.ds(p, lines, stride=gl), :] = value
    for j in range(plan.subj):
        for t in range(plan.tiles):
            start = (j * plan.tiles + t) * gl
            out_ref[j, :, t * lane : (t + 1) * lane] = y_ref[start : start + gl, :]


def late_backward(plan, place, f, ends):
    return call_once(
        functools.partial(late_backward_kernel, plan),
        "first_and_back",
        jax.ShapeDtypeStruct((plan.subj, plan.gl, plan.lanes), jnp.float32),
        place,
        [plan.r_late, plan.g_table, f, *ends],
        scratch=[
            pltpu.VMEM(f.shape, jnp.float32),
            pltpu.VMEM((plan.length // plan.ty * plan.gl, lane), jnp.float32),
        ],
    )


def finish_kernel(plan, y_step, place_ref, i_ref, velocity, *rest):
    pieces, out = rest[:-1], rest[-1]
    length, xl = plan.length, plan.xl
    me = place_ref[plan.at_space]
    starts = [pl.multiple_of((me ^ d) * plan.g, 8) for d in range(plan.space)]
    high, low = (
        jnp.concatenate(
            [i_ref[i, pl.ds(start, plan.g), :] for start in starts] + [i_ref[i, plan.early :, :]],
            axis=0,
        )
        for i in range(2)
    )
    table = jnp.concatenate([high, high, low], axis=0)
    lines = []
    for t in range(y_step // plan.ty):
        columns = jnp.concatenate([p[:, t * lane : (t + 1) * lane] for p in pieces], axis=0)
        high, low = split(columns.T)
        both = jnp.concatenate([high, low, high], axis=1)
        lines.append(jnp.dot(both, table, preferred_element_type=jnp.float32))
        if len(lines) * plan.ty == 8:
            y = (t + 1) * plan.ty - 8
            block = jnp.concatenate(lines, axis=0).reshape(8, xl, length)
            smoothed = jnp.swapaxes(block, 0, 1)
            vel = velocity[:, y : y + 8, :]
            out[:, y : y + 8, :] = vel - step_size * (2.0 * vel - smoothed)
            lines = []


def finish(plan, place, velocity, pieces):
    xl, yl, length = velocity.shape
    y_step = 16
    width = y_step * xl
    block = pl.BlockSpec((xl, y_step, length), lambda at, place: (0, at, 0))
    return pl.pallas_call(
        functools.partial(finish_kernel, plan, y_step),
        out_shape=jax.ShapeDtypeStruct(velocity.shape, jnp.float32),
        grid_spec=pltpu.PrefetchScalarGridSpec(
            num_scalar_prefetch=1,
            grid=(yl // y_step,),
            in_specs=[
                pl.BlockSpec((2, length, length), lambda at, place: (0, 0, 0)),
                block,
            ]
            + [pl.BlockSpec((p.shape[0], width), lambda at, place: (0, at)) for p in pieces],
            out_specs=block,
        ),
        compiler_params=params(),
        name="last_back",
    )(place, jnp.asarray(plan.i_table), velocity, *pieces)


def tie(first, second):
    return lax.optimization_barrier((first, second))


def over_one(plan, part, d):
    if d == 0:
        return part
    return lax.ppermute(part, "space", [(i, i ^ d) for i in range(plan.space)])


def over_space(plan, pieces):
    return [over_one(plan, piece, d) for d, piece in enumerate(pieces)]


def ring_body(plan, template_warped, subject_images, jacobians, velocity):
    subj, space, half = plan.subj, plan.space, plan.subj // 2
    j, s = lax.axis_index("subj"), lax.axis_index("space")
    table = plan.place_table
    place = lax.dynamic_slice(jnp.asarray(table), (j, s, 0), (1, 1, table.shape[2])).reshape(-1)
    to_right = [(plan.ring[i], plan.ring[(i + 1) % subj]) for i in range(subj)]
    to_left = [(b, a) for a, b in to_right]

    def go_round(both):
        return lax.ppermute(both[0], "subj", to_right), lax.ppermute(both[1], "subj", to_left)

    local = [
        force_blocks(plan, k, place, template_warped, subject_images, jacobians)
        for k in range(subj)
    ]

    parts = range(early_parts)
    streams = [(local[0][0][p], local[0][1][p]) for p in parts]
    for k in range(1, subj):
        streams = [go_round(both) for both in streams]
        if k < subj - 1:
            streams = [
                tuple(b + local[k][way][p] for way, b in enumerate(both))
                for p, both in enumerate(streams)
            ]
    late = regroup(plan, place, [local[k][way][-1] for k in range(subj) for way in range(2)])
    both, streams = tie((late[0][0], late[1][0]), streams)
    pieces = join(
        plan, place, [a for p in parts for way in range(2) for a in (local[-1][way][p], streams[p][way])]
    )

    top = space // 2
    far = lax.ppermute(
        jnp.concatenate(pieces[top:]), "space", [(i, i ^ top) for i in range(space)]
    )
    moved = over_space(plan, pieces[:top])
    arrived = []
    for k in range(1, subj):
        if k == near_step:
            both, moved = tie(both, moved)
        if k == far_step:
            far = over_space(plan, [far[d * plan.g : (d + 1) * plan.g] for d in range(top)])
            both, far = tie(both, far)
            f, ends = forward_lines(plan, place, [*moved, *far])
        if k >= ends_step and len(arrived) < half:
            extra = arrived[-1] if arrived else (ends, ends)
            both = tuple(jnp.concatenate([b, e]) for b, e in zip(both, extra))
        both = go_round(both)
        if both[0].shape[0] > plan.late:
            arrived.append(tuple(b[plan.late :] for b in both))
        if k == far_step:
            both, (f, ends) = tie(both, (f, ends))
        if k < subj - 1:
            both = tuple(b[: plan.late] + late[way][k] for way, b in enumerate(both))
    while len(arrived) < half:
        arrived.append(go_round(arrived[-1] if arrived else (ends, ends)))
    all_ends = [ends] + [e for pair in arrived for e in pair]

    f_late, ends_late = late_forward(
        plan, place, late[0][subj - 1 :], late[1][subj - 1 :], *both
    )
    others = [over_one(plan, ends_late, d) for d in range(space)]
    f, others = tie(f, others)
    *back, far = backward_lines(plan, place, f, all_ends[:subj])
    f_late, back[0] = tie(f_late, back[0])
    far = lax.ppermute(far, "space", [(i, i ^ top) for i in range(space)])
    back = over_space(plan, back)
    back_late = late_backward(plan, place, f_late, others)
    back_late, back = tie(back_late, back)
    back_late = lax.all_to_all(back_late, "subj", 0, 0)
    back_late = back_late.reshape(plan.late, plan.lanes)
    far = [far[d * plan.g : (d + 1) * plan.g] for d in range(top)]
    back += over_space(plan, far)
    return finish(plan, place, velocity, [*back, back_late])


def smoothing_symbol(first, second, third, length):
    def damping(freq):
        turns = (freq % length).astype(jnp.float32)
        return 2.0 - 2.0 * jnp.cos(turns * (2.0 * math.pi / length))

    total = damping(first) + damping(second) + damping(third)
    return 1.0 / (1.0 + alpha_reach * total) ** 2


def transposing_body(template_warped, subject_images, jacobians, velocity):
    length = template_warped.shape[3]
    half = length // 2
    warped = template_warped.astype(jnp.float32)
    slope = (jnp.roll(warped, -1, axis=3) - jnp.roll(warped, 1, axis=3)) * 0.5
    partial_value = jnp.sum(
        jacobians.astype(jnp.float32) * (subject_images.astype(jnp.float32) - warped) * slope,
        axis=0,
    )
    forward, inverse, _ = packed_np(length)
    forward, inverse = forward.astype(np.float32), inverse.astype(np.float32)
    packed = jnp.einsum("xyz,zp->xpy", partial_value, forward, precision=highest)
    packed = lax.psum_scatter(packed, "subj", scatter_dimension=1, tiled=True)
    packed = packed * (2.0 / sigma_sq)
    spectra = jnp.einsum("xpy,yk->kpx", packed, forward, precision=highest)
    lines = lax.all_to_all(spectra, "space", split_axis=0, concat_axis=2, tiled=True)
    freq_lines = jnp.einsum("kpx,xw->kpw", lines, forward, precision=highest)

    def true_freq(index):
        return jnp.where(index <= half, index, index - half)

    def mine(axis, size):
        return true_freq(lax.axis_index(axis) * size + jnp.arange(size, dtype=jnp.int32))

    symbol = smoothing_symbol(
        mine("space", lines.shape[0])[:, None, None],
        mine("subj", lines.shape[1])[None, :, None],
        true_freq(jnp.arange(length, dtype=jnp.int32))[None, None, :],
        length,
    )
    back_lines = jnp.einsum("kpw,wx->xpk", freq_lines * symbol, inverse, precision=highest)
    columns = lax.all_to_all(back_lines, "space", split_axis=0, concat_axis=2, tiled=True)
    real_field = jnp.einsum("xpk,ky->xpy", columns, inverse, precision=highest)
    depth_lines = lax.all_to_all(real_field, "subj", split_axis=2, concat_axis=1, tiled=True)
    smoothed = jnp.einsum("xpy,pz->xyz", depth_lines, inverse, precision=highest)
    return velocity - step_size * (2.0 * velocity - smoothed)


def body(subj, space, template_warped, subject_images, jacobians, velocity):
    _, xl, _, length = template_warped.shape
    yl = velocity.shape[1]
    power_of_two = subj & (subj - 1) == 0 and space & (space - 1) == 0
    fits = (
        subj > 1
        and power_of_two
        and length % lane == 0
        and yl % 32 == 0
        and xl >= 16
        and lane % xl == 0
        and 2 * xl == lane
        and early_eighths * length // 8 % (16 * space) == 0
        and space % early_parts == 0
        and early_eighths * length // 8 % (8 * space) == 0
        and (8 - early_eighths) * length // 8 % (8 * subj) == 0
        and yl * xl == 8 * length
    )
    if not fits:
        return transposing_body(template_warped, subject_images, jacobians, velocity)
    plan = Plan(length, xl, subj, space)
    return ring_body(plan, template_warped, subject_images, jacobians, velocity)


def solution(mesh):
    return jax.shard_map(
        functools.partial(body, mesh.shape["subj"], mesh.shape["space"]),
        mesh=mesh,
        in_specs=(
            P("subj", "space", None, None),
            P("subj", "space", None, None),
            P("subj", "space", None, None),
            P("space", "subj", None),
        ),
        out_specs=P("space", "subj", None),
        check_vma=False,
    )
```
